128 devices in a mesh: row: 16 (over z, y), col: 8 (over x, core).
Axes of the slice: x: 4, y: 4, z: 4, core: 2. Of those that a mesh axis runs over, the one named last changes fastest.
Arguments:
- image: bfloat16 [64, 64, 6144], P('row', None, 'col'), may hold values from -8 to 8
- filter_bank: float32 [2, 64, 64, 6144], P(None, None, 'row', 'col'), may hold values from -6 to 6
- gain_first: float32 [6144], P('col'), may hold values from 0.1 to 1.9
- gain_second: float32 [6144], P('col'), may hold values from 0.1 to 1.9
- w_in: bfloat16 [6144, 24576], P('col', 'row'), may hold values from -0.078125 to 0.078125
- b_in: float32 [24576], P('row'), may hold values from -4 to 4
- w_out: bfloat16 [24576, 6144], P('row', 'col'), may hold values from -0.0390625 to 0.0390625
- b_out: float32 [6144], P('col'), may hold values from -3 to 3
Outputs:
- block_out: bfloat16 [64, 64, 6144], P('row', None, 'col')
The draws below stay inside these ranges and needn't reach their ends.
All inputs are finite; a program needn't handle non-finite values.
Results may differ from the reference program's by a relative error of at most 0.017.
Values may be sent and summed in bfloat16 or wider, within the bound.
No kernel may reach another device: no remote copies, remote signals or barrier semaphores. Data moves between devices by JAX's collectives and lax.ppermute only.
A program may use at most 128 MiB of HBM per device.

```python
import math
import jax
import jax.numpy as jnp
from jax import lax

H = 64
W = 64
D = 6144
FF = 24576
N_ROW = 16
N_COL = 8


def draw_image(key, part):
    key_base = jax.random.fold_in(key, 11)
    key_chan = jax.random.fold_in(key, 12)
    key_tok = jax.random.fold_in(key, 13)
    channel = jnp.arange(D, dtype=jnp.int32).astype(jnp.float32)
    rise = 0.5 * jnp.exp(jnp.log(3.0) * channel / (D - 1))
    rough = jnp.exp(jax.random.uniform(key_chan, (D,), jnp.float32, -0.7, 0.7))
    base = jax.random.normal(key_base, (H, W, D), jnp.float32)
    token_scale = jnp.exp(jax.random.uniform(key_tok, (H, W, 1), jnp.float32, -0.7, 0.7))
    values = base * rise * rough * token_scale
    return jnp.clip(values, -8.0, 8.0).astype(jnp.bfloat16)


def block_scale(rng, shape, split, low, largest):
    def one(axis_at, parts):
        draws = jax.random.uniform(jax.random.fold_in(jax.random.fold_in(rng, 6), axis_at), (parts,), jnp.float32, low / len(split), largest / len(split))
        return jnp.repeat(jnp.exp(draws), shape[axis_at] // parts).reshape((-1,) + (1,) * (len(shape) - axis_at - 1))

    level = one(*split[0])
    for cut in split[1:]:
        level = level * one(*cut)
    return level


def noise(key, shape, width, reach, shards=(), kind=jnp.bfloat16):
    level = block_scale(key, shape, shards, -0.22, 0.18) if shards else 1.0
    entries = jax.random.normal(key, shape, jnp.float32) * width * level
    return jnp.minimum(jnp.maximum(entries, -reach), reach).astype(kind)


def setup_inputs(seed: int = 0) -> dict:
    splits = jax.random.split(jax.random.key(seed), 9)
    return {
        "image": draw_image(jax.random.fold_in(splits[8], 71), 0),
        "filter_bank": noise(splits[1], (2, H, W, D), 1.0, 6.0, ((2, 16), (3, 8)), jnp.float32),
        "gain_first": jnp.clip(1.0 + 0.18 * jax.random.normal(splits[2], (D,), jnp.float32), 0.1, 1.9),
        "gain_second": jnp.clip(1.0 + 0.18 * jax.random.normal(splits[3], (D,), jnp.float32), 0.1, 1.9),
        "w_in": noise(splits[4], (D, FF), D ** -0.5, 0.078125, ((0, 8), (1, 16))),
        "b_in": noise(splits[5], (FF,), 1.0, 4.0, ((0, 16),), jnp.float32),
        "w_out": noise(splits[6], (FF, D), FF ** -0.5, 0.0390625, ((0, 16), (1, 8))),
        "b_out": noise(splits[7], (D,), 0.5, 3.0, ((0, 8),), jnp.float32),
    }


def norm_rows(values):
    mean = lax.optimization_barrier(jnp.sum(values, axis=-1, keepdims=True)) / D
    square = lax.optimization_barrier(jnp.sum(values * values, axis=-1, keepdims=True)) / D
    return (values - mean) / jnp.sqrt(square - mean * mean + 1e-05)

def tables(count):
    index = jnp.arange(count, dtype=jnp.int32)
    angle = (index[:, None] * index[None, :] % count).astype(jnp.float32) * (2.0 * math.pi / count)
    return (jnp.cos(angle), jnp.sin(angle))

def reference(image, filter_bank, gain_first, gain_second, w_in, b_in, w_out, b_out):
    high = lax.Precision.HIGHEST
    source = image.astype(jnp.float32)
    normed = norm_rows(source) * gain_first
    cos_w, sin_w = tables(W)
    cos_h, sin_h = tables(H)
    col_re = jnp.einsum('rcd,ck->rkd', normed, cos_w, precision=high)
    col_im = -jnp.einsum('rcd,ck->rkd', normed, sin_w, precision=high)
    spec_re = jnp.einsum('rn,rkd->nkd', cos_h, col_re, precision=high) + jnp.einsum('rn,rkd->nkd', sin_h, col_im, precision=high)
    spec_im = jnp.einsum('rn,rkd->nkd', cos_h, col_im, precision=high) - jnp.einsum('rn,rkd->nkd', sin_h, col_re, precision=high)
    filt_re = filter_bank[0] * spec_re - filter_bank[1] * spec_im
    filt_im = filter_bank[0] * spec_im + filter_bank[1] * spec_re
    back_re = jnp.einsum('nr,nkd->rkd', cos_h, filt_re, precision=high) - jnp.einsum('nr,nkd->rkd', sin_h, filt_im, precision=high)
    back_im = jnp.einsum('nr,nkd->rkd', sin_h, filt_re, precision=high) + jnp.einsum('nr,nkd->rkd', cos_h, filt_im, precision=high)
    mixed = (jnp.einsum('rkd,kc->rcd', back_re, cos_w, precision=high) - jnp.einsum('rkd,kc->rcd', back_im, sin_w, precision=high)) / (H * W)
    resid = (source + mixed).reshape(H * W, D)
    act = (norm_rows(resid) * gain_second).astype(jnp.bfloat16)
    block_d = D // N_COL
    pre = jnp.zeros((H * W, FF), jnp.float32)
    for part_index in range(N_COL):
        piece = jnp.dot(act[:, part_index * block_d:(part_index + 1) * block_d], w_in[part_index * block_d:(part_index + 1) * block_d, :], preferred_element_type=jnp.float32)
        piece = lax.optimization_barrier(piece.astype(jnp.bfloat16))
        pre = pre + piece.astype(jnp.float32)
    hidden = jax.nn.gelu(pre + b_in, approximate=False).astype(jnp.bfloat16)
    block_f = FF // N_ROW
    proj = jnp.zeros((H * W, D), jnp.float32)
    for part_index in range(N_ROW):
        piece = jnp.dot(hidden[:, part_index * block_f:(part_index + 1) * block_f], w_out[part_index * block_f:(part_index + 1) * block_f, :], preferred_element_type=jnp.float32)
        piece = lax.optimization_barrier(piece.astype(jnp.bfloat16))
        proj = proj + piece.astype(jnp.float32)
    result = (resid + proj + b_out).astype(jnp.bfloat16)
    return result.reshape(H, W, D)
```

```python
import math

import jax
import jax.numpy as jnp
from jax import lax
from jax.sharding import PartitionSpec as P

SIDE = 4
BF = jnp.bfloat16
F32 = jnp.float32


def tables(count):
    index = jnp.arange(count, dtype=jnp.int32)
    angle = (index[:, None] * index[None, :] % count).astype(jnp.float32) * (2.0 * math.pi / count)
    return (jnp.cos(angle), jnp.sin(angle))


def finish_norm(values, totals, width_all):
    mean = totals[0][..., None] / width_all
    square = totals[1][..., None] / width_all
    return (values - mean) / jnp.sqrt(square - mean * mean + 1e-05)


def shift_row(a, dz, dy):
    pairs = []
    for z in range(SIDE):
        for y in range(SIDE):
            pairs.append((z * SIDE + y, (z + dz) % SIDE * SIDE + (y + dy) % SIDE))
    return lax.ppermute(a, "row", pairs)


def along(a, axis, step):
    return shift_row(a, step, 0) if axis == "z" else shift_row(a, 0, step)


def gather_axis(a, axis):
    return jnp.stack([a, along(a, axis, 1), along(a, axis, -1), along(a, axis, 2)])


BACK = (0, -1, 1, 2)


def reduce_axis(a, axis):
    total = a[0].astype(F32)
    for i in (1, 2, 3):
        total = total + along(a[i], axis, BACK[i]).astype(F32)
    return total


def spectral(image, filter_bank, gain_first, gain_second):
    high = lax.Precision.HIGHEST
    rows_here, width, chans = image.shape
    height = rows_here * lax.axis_size("row")
    cols = lax.axis_size("col")
    width_all = chans * cols
    source = image.astype(jnp.float32)
    place = lax.broadcasted_iota(jnp.int32, (cols, 1), 0) == lax.axis_index("col")
    spread = jnp.where(place, gain_second[None, :], 0.0)
    sums, squares, gains = lax.psum(
        (jnp.sum(source, axis=-1), jnp.sum(source * source, axis=-1), spread), "col"
    )
    normed = finish_norm(source, (sums, squares), width_all) * gain_first
    cos_w, sin_w = tables(width)
    cos_h, sin_h = tables(height)
    col_re = jnp.einsum("rcd,ck->rkd", normed, cos_w, precision=high)
    col_im = -jnp.einsum("rcd,ck->rkd", normed, sin_w, precision=high)
    col_re, col_im = (
        lax.all_to_all(
            col_re.astype(jnp.bfloat16), "row", split_axis=1, concat_axis=0, tiled=True
        ).astype(col_re.dtype),
        lax.all_to_all(
            col_im.astype(jnp.bfloat16), "row", split_axis=1, concat_axis=0, tiled=True
        ).astype(col_im.dtype),
    )
    spec_re = jnp.einsum("rn,rkd->nkd", cos_h, col_re, precision=high) + jnp.einsum(
        "rn,rkd->nkd", sin_h, col_im, precision=high
    )
    spec_im = jnp.einsum("rn,rkd->nkd", cos_h, col_im, precision=high) - jnp.einsum(
        "rn,rkd->nkd", sin_h, col_re, precision=high
    )
    filt_re = filter_bank[0] * spec_re - filter_bank[1] * spec_im
    filt_im = filter_bank[0] * spec_im + filter_bank[1] * spec_re
    back_re = jnp.einsum("nr,nkd->rkd", cos_h, filt_re, precision=high) - jnp.einsum(
        "nr,nkd->rkd", sin_h, filt_im, precision=high
    )
    back_im = jnp.einsum("nr,nkd->rkd", sin_h, filt_re, precision=high) + jnp.einsum(
        "nr,nkd->rkd", cos_h, filt_im, precision=high
    )
    back_re, back_im = (
        lax.all_to_all(
            back_re.astype(jnp.bfloat16), "row", split_axis=0, concat_axis=1, tiled=True
        ).astype(back_re.dtype),
        lax.all_to_all(
            back_im.astype(jnp.bfloat16), "row", split_axis=0, concat_axis=1, tiled=True
        ).astype(back_im.dtype),
    )
    mixed = (
        jnp.einsum("rkd,kc->rcd", back_re, cos_w, precision=high)
        - jnp.einsum("rkd,kc->rcd", back_im, sin_w, precision=high)
    ) / (height * width)
    return (source + mixed).reshape(rows_here * width, chans), gains


def on_device(image, filter_bank, gain_first, gain_second, w_in, b_in, w_out, b_out):
    rows_here, width, chans = image.shape
    cols = lax.axis_size("col")
    width_all = chans * cols
    w_in_all = lax.all_gather(w_in, "col", axis=0, tiled=True)
    w_out_all = lax.all_gather(w_out, "col", axis=0, tiled=False)
    resid, gains = spectral(image, filter_bank, gain_first, gain_second)
    tokens = rows_here * width
    own = tokens // cols
    moved = lax.all_to_all(
        resid.astype(BF).reshape(cols, own, chans), "col", split_axis=0, concat_axis=0, tiled=True
    ).astype(F32)
    totals = (jnp.sum(moved, axis=(0, 2)), jnp.sum(moved * moved, axis=(0, 2)))
    mean = totals[0][None, :, None] / width_all
    square = totals[1][None, :, None] / width_all
    act = (moved - mean) / jnp.sqrt(square - mean * mean + 1e-05) * gains[:, None, :]
    act = act.astype(BF).transpose(1, 0, 2).reshape(own, width_all)
    half = own // 2
    first = gather_axis(gather_axis(act[:half], "z"), "y")
    second = gather_axis(gather_axis(act[half:], "y"), "z")
    hiddens = []
    for part in (first, second):
        pre = jnp.dot(
            part.reshape(-1, width_all), w_in_all, preferred_element_type=jnp.float32
        )
        hiddens.append(jax.nn.gelu(pre + b_in, approximate=False).astype(BF))
    parts = []
    for hid, axes in zip(hiddens, (("y", "z"), ("z", "y"))):
        out = jnp.einsum("tf,jfd->tjd", hid, w_out_all, preferred_element_type=jnp.float32)
        out = out.astype(BF).reshape(SIDE, SIDE, half, width_all)
        for axis in axes:
            out = reduce_axis(out, axis).astype(BF)
        parts.append(out)
    proj = jnp.concatenate(parts, axis=0).reshape(own, cols, chans).transpose(1, 0, 2)
    proj = lax.all_to_all(proj, "col", split_axis=0, concat_axis=0, tiled=True)
    result = (resid + proj.reshape(tokens, chans).astype(F32) + b_out).astype(BF)
    return result.reshape(rows_here, width, chans)


def solution(mesh):
    placed = (
        P("row", None, "col"),
        P(None, None, "row", "col"),
        P("col"),
        P("col"),
        P("col", "row"),
        P("row"),
        P("row", "col"),
        P("col"),
    )
    return jax.shard_map(
        on_device, mesh=mesh, in_specs=placed, out_specs=P("row", None, "col"), check_vma=False
    )
```

```python
import functools
import math

import jax
import jax.numpy as jnp
import numpy as np
from jax import lax
from jax.experimental import pallas as pl
from jax.experimental.pallas import tpu as pltpu
from jax.sharding import PartitionSpec as P

SIDE = 4
BF = jnp.bfloat16
F32 = jnp.float32
MB = 1 << 20


def angles(count):
    index = np.arange(count)
    turn = (index[:, None] * index[None, :]) % count * (2.0 * math.pi / count)
    return np.cos(turn), np.sin(turn)


def spectral_tables(here, width, height):
    groups = height // here
    per = width // groups
    cos_w, sin_w = angles(width)
    cos_h, sin_h = angles(height)
    eye_r, eye_k = np.eye(here), np.eye(per)
    out = np.stack([cos_w, -sin_w]).reshape(2, width, groups, per)
    one = np.einsum("scqk,rt->qrsktc", out, eye_r).reshape(2 * here * width, here * width)
    turn = np.stack([np.stack([cos_h, sin_h]), np.stack([-sin_h, cos_h])])
    turn = turn.reshape(2, 2, groups, here, height)
    two = np.einsum("uvqrn,kl->unkqrvl", turn, eye_k).reshape(2 * height * per, 2 * height * per)
    back = np.stack([np.stack([cos_h, -sin_h]), np.stack([sin_h, cos_h])])
    back = back.reshape(2, 2, height, groups, here)
    three = np.einsum("uvnqr,kl->qrukvnl", back, eye_k).reshape(2 * height * per, 2 * height * per)
    four = np.einsum("sqkc,rt->rcqtsk", out.transpose(0, 2, 3, 1), eye_r)
    four = four.reshape(here * width, 2 * here * width) / (width * height)
    return [t.astype(np.float32) for t in (one, two, three, four)]


def shift_row(a, dz, dy):
    pairs = []
    for z in range(SIDE):
        for y in range(SIDE):
            pairs.append((z * SIDE + y, (z + dz) % SIDE * SIDE + (y + dy) % SIDE))
    return lax.ppermute(a, "row", pairs)


def along(a, axis, step):
    return shift_row(a, step, 0) if axis == "z" else shift_row(a, 0, step)


def params(mb):
    return pltpu.CompilerParams(vmem_limit_bytes=mb * MB)


def act_kernel(moved_ref, first_ref, second_ref):
    cols, rows, chans = moved_ref.shape
    half = first_ref.shape[0]
    values = moved_ref[:, : 2 * half, :].astype(F32)
    gains = jnp.sum(moved_ref[:, 2 * half :, :].astype(F32)[:, :3], axis=1)
    mean = jnp.sum(jnp.sum(values, axis=0), axis=-1, keepdims=True) / (cols * chans)
    square = jnp.sum(jnp.sum(values * values, axis=0), axis=-1, keepdims=True) / (cols * chans)
    scale = 1.0 / jnp.sqrt(square - mean * mean + 1e-05)
    for j in range(cols):
        part = ((values[j] - mean) * scale * gains[j][None, :]).astype(BF)
        first_ref[:, j * chans : (j + 1) * chans] = part[:half]
        second_ref[:, j * chans : (j + 1) * chans] = part[half:]


def normalize(moved, half):
    cols, _, chans = moved.shape
    shape = jax.ShapeDtypeStruct((half, cols * chans), BF)
    return pl.pallas_call(act_kernel, out_shape=(shape, shape), compiler_params=params(16))(moved)


def mm1_kernel(block, *refs):
    pieces, (w_ref, b_ref, o_ref) = refs[:-3], refs[-3:]
    depth = w_ref.shape[0]
    total = None
    for at in range(0, depth, block):
        left = jnp.concatenate(
            [p[:, :, at : at + block].reshape(-1, block) for p in pieces], axis=0
        )
        term = jnp.dot(left, w_ref[at : at + block, :], preferred_element_type=F32)
        total = term if total is None else total + term
    pre = total + b_ref[...]
    o_ref[...] = (0.5 * pre * (1.0 + lax.erf(pre * math.sqrt(0.5)))).astype(BF)


def matmul_in(pieces, w, b):
    depth, width = w.shape
    shape = pieces[0].shape
    tokens = len(pieces) * shape[0] * shape[1]
    tile = 256
    return pl.pallas_call(
        functools.partial(mm1_kernel, 768),
        grid=(width // tile,),
        in_specs=[pl.BlockSpec(shape, lambda i: (0, 0, 0)) for _ in pieces]
        + [
            pl.BlockSpec((depth, tile), lambda i: (0, i)),
            pl.BlockSpec((1, tile), lambda i: (0, i)),
        ],
        out_specs=pl.BlockSpec((tokens, tile), lambda i: (0, i)),
        out_shape=jax.ShapeDtypeStruct((tokens, width), BF),
        compiler_params=params(40),
        cost_estimate=pl.CostEstimate(
            flops=2 * tokens * depth * width,
            bytes_accessed=2 * (tokens * depth + depth * width),
            transcendentals=0,
        ),
    )(*pieces, w, b[None])


def mm2_kernel(h_ref, w_ref, *outs):
    out = jnp.dot(h_ref[...], w_ref[0], preferred_element_type=F32)
    shape = outs[0].shape
    rows = shape[0] * shape[1]
    for i, o_ref in enumerate(outs):
        o_ref[...] = out[i * rows : (i + 1) * rows].astype(BF).reshape(shape)


def matmul_out(hidden, w, half):
    cols, depth, chans = w.shape
    tokens = hidden.shape[0]
    count = tokens // (SIDE * half)
    return pl.pallas_call(
        mm2_kernel,
        grid=(cols,),
        in_specs=[
            pl.BlockSpec((tokens, depth), lambda j: (0, 0)),
            pl.BlockSpec((1, depth, chans), lambda j: (j, 0, 0)),
        ],
        out_specs=[pl.BlockSpec((SIDE, half, chans), lambda j: (0, 0, j))] * count,
        out_shape=[jax.ShapeDtypeStruct((SIDE, half, cols * chans), BF)] * count,
        compiler_params=params(40),
        cost_estimate=pl.CostEstimate(
            flops=2 * tokens * depth * cols * chans,
            bytes_accessed=2 * (tokens * depth + depth * cols * chans + tokens * cols * chans),
            transcendentals=0,
        ),
    )(hidden, w)


def add_kernel(a, b, c, d, *outs):
    total = (a[...].astype(F32) + b[...].astype(F32)) + (c[...].astype(F32) + d[...].astype(F32))
    for i, o_ref in enumerate(outs):
        o_ref[...] = total[i].astype(BF)


def add_pieces(parts):
    count, half, width = parts[0].shape
    tile = width // 4
    return pl.pallas_call(
        add_kernel,
        grid=(width // tile,),
        in_specs=[pl.BlockSpec((count, half, tile), lambda j: (0, 0, j))] * len(parts),
        out_specs=[pl.BlockSpec((half, tile), lambda j: (0, j))] * count,
        out_shape=[jax.ShapeDtypeStruct((half, width), BF)] * count,
        compiler_params=params(16),
    )(*parts)


def last_kernel(a, b, c, d, e, f, g, h, o_ref):
    half = a.shape[0]
    top = (a[...].astype(F32) + b[...].astype(F32)) + (c[...].astype(F32) + d[...].astype(F32))
    low = (e[...].astype(F32) + f[...].astype(F32)) + (g[...].astype(F32) + h[...].astype(F32))
    o_ref[0, :half, :] = top.astype(BF)
    o_ref[0, half:, :] = low.astype(BF)


def add_last(first, second, cols):
    half, width = first[0].shape
    chans = width // cols
    return pl.pallas_call(
        last_kernel,
        grid=(cols,),
        in_specs=[pl.BlockSpec((half, chans), lambda j: (0, j))] * 8,
        out_specs=pl.BlockSpec((1, 2 * half, chans), lambda j: (j, 0, 0)),
        out_shape=jax.ShapeDtypeStruct((cols, 2 * half, chans), BF),
        compiler_params=params(16),
    )(*first, *second)


def exchange(a, axis):
    return lax.all_to_all(a, axis, split_axis=0, concat_axis=0, tiled=True)


def spectral(image, filter_bank, gain_first):
    rows_here, width, chans = image.shape
    groups = lax.axis_size("row")
    width_all = chans * lax.axis_size("col")
    tokens = rows_here * width
    one, two, three, four = spectral_tables(rows_here, width, rows_here * groups)
    high = lax.Precision.HIGH
    source = image.astype(F32).reshape(tokens, chans)
    sums, squares = lax.psum(
        (jnp.sum(source, axis=-1), jnp.sum(source * source, axis=-1)), "col"
    )
    mean = sums[:, None] / width_all
    square = squares[:, None] / width_all
    normed = (source - mean) / jnp.sqrt(square - mean * mean + 1e-05) * gain_first
    col = jnp.dot(one, normed, precision=high).astype(BF)
    col = exchange(col.reshape(groups, -1, chans), "row").reshape(-1, chans)
    spec = jnp.dot(two, col.astype(F32), precision=high)
    split = spec.shape[0] // 2
    spec_re, spec_im = spec[:split], spec[split:]
    f_re, f_im = filter_bank[0].reshape(-1, chans), filter_bank[1].reshape(-1, chans)
    filt = jnp.concatenate(
        [f_re * spec_re - f_im * spec_im, f_re * spec_im + f_im * spec_re], axis=0
    )
    back = jnp.dot(three, filt, precision=high).astype(BF)
    back = exchange(back.reshape(groups, -1, chans), "row").reshape(-1, chans)
    return source + jnp.dot(four, back.astype(F32), precision=high)


def three_parts(gain):
    top = lax.reduce_precision(gain, 8, 7)
    mid = lax.reduce_precision(gain - top, 8, 7)
    return jnp.stack([top, mid, gain - top - mid]).astype(BF)


def gather_two(a, axis_one, axis_two):
    got = jnp.stack([a] + [along(a, axis_one, s) for s in (1, -1, 2)])
    return [got] + [along(got, axis_two, s) for s in (1, -1, 2)]


def send_back(parts, axis):
    return [parts[0]] + [along(p, axis, s) for p, s in zip(parts[1:], (-1, 1, 2))]


def on_device(image, filter_bank, gain_first, gain_second, w_in, b_in, w_out, b_out):
    rows_here, width, chans = image.shape
    cols = lax.axis_size("col")
    w_in_all = lax.all_gather(w_in, "col", axis=0, tiled=True)
    w_out_all = lax.all_gather(w_out, "col", axis=0, tiled=False)
    resid = spectral(image, filter_bank, gain_first)
    tokens = rows_here * width
    own = tokens // cols
    half = own // 2
    extra = jnp.pad(three_parts(gain_second), ((0, half - 3), (0, 0)))
    message = jnp.concatenate(
        [
            resid.astype(BF).reshape(cols, own, chans),
            jnp.broadcast_to(extra[None], (cols, half, chans)),
        ],
        axis=1,
    )
    first, second = normalize(exchange(message, "col"), half)
    pieces = gather_two(first, "z", "y") + gather_two(second, "y", "z")
    hidden = matmul_in(pieces, w_in_all, b_in)
    outs = matmul_out(hidden, w_out_all, half)
    count = len(outs) // 2
    first = send_back(add_pieces(send_back(outs[:count], "y")), "z")
    second = send_back(add_pieces(send_back(outs[count:], "z")), "y")
    proj = exchange(add_last(first, second, cols), "col")
    result = (resid + proj.reshape(tokens, chans).astype(F32) + b_out).astype(BF)
    return result.reshape(rows_here, width, chans)


def solution(mesh):
    placed = (
        P("row", None, "col"),
        P(None, None, "row", "col"),
        P("col"),
        P("col"),
        P("col", "row"),
        P("row"),
        P("row", "col"),
        P("col"),
    )
    return jax.shard_map(
        on_device, mesh=mesh, in_specs=placed, out_specs=P("row", None, "col"), check_vma=False
    )
```

```python
import functools
import math

import jax
import jax.numpy as jnp
import numpy as np
from jax import lax
from jax.experimental import pallas as pl
from jax.experimental.pallas import tpu as pltpu
from jax.sharding import PartitionSpec as P

SIDE = 4
BF = jnp.bfloat16
F32 = jnp.float32
MB = 1 << 20


def angles(count):
    index = np.arange(count)
    turn = (index[:, None] * index[None, :]) % count * (2.0 * math.pi / count)
    return np.cos(turn), np.sin(turn)


def spectral_tables(here, width, height):
    groups = height // here
    per = width // groups
    cos_w, sin_w = angles(width)
    cos_h, sin_h = angles(height)
    eye_r, eye_k = np.eye(here), np.eye(per)
    out = np.stack([cos_w, -sin_w]).reshape(2, width, groups, per)
    one = np.einsum("scqk,rt->qrsktc", out, eye_r).reshape(2 * here * width, here * width)
    turn = np.stack([np.stack([cos_h, sin_h]), np.stack([-sin_h, cos_h])])
    turn = turn.reshape(2, 2, groups, here, height)
    two = np.einsum("uvqrn,kl->unkqrvl", turn, eye_k).reshape(2 * height * per, 2 * height * per)
    back = np.stack([np.stack([cos_h, -sin_h]), np.stack([sin_h, cos_h])])
    back = back.reshape(2, 2, height, groups, here)
    three = np.einsum("uvnqr,kl->qrukvnl", back, eye_k).reshape(2 * height * per, 2 * height * per)
    four = np.einsum("sqkc,rt->rcqtsk", out.transpose(0, 2, 3, 1), eye_r)
    four = four.reshape(here * width, 2 * here * width) / (width * height)
    return [t.astype(np.float32) for t in (one, two, three, four)]


def shift_row(a, dz, dy):
    pairs = []
    for z in range(SIDE):
        for y in range(SIDE):
            pairs.append((z * SIDE + y, (z + dz) % SIDE * SIDE + (y + dy) % SIDE))
    return lax.ppermute(a, "row", pairs)


def shift_col(a, dx, dc):
    pairs = []
    for x in range(SIDE):
        for core in range(2):
            pairs.append((x * 2 + core, (x + dx) % SIDE * 2 + (core ^ dc)))
    return lax.ppermute(a, "col", pairs)


def along(a, axis, step):
    return shift_row(a, step, 0) if axis == "z" else shift_row(a, 0, step)


def params(mb):
    return pltpu.CompilerParams(vmem_limit_bytes=mb * MB)


def act_kernel(order_ref, moved_ref, gain_ref, first_ref, second_ref):
    cols, _, chans = moved_ref.shape
    half = first_ref.shape[0]
    values = moved_ref[...].astype(F32)
    mean = jnp.sum(jnp.sum(values, axis=0), axis=-1, keepdims=True) / (cols * chans)
    square = jnp.sum(jnp.sum(values * values, axis=0), axis=-1, keepdims=True) / (cols * chans)
    scale = 1.0 / jnp.sqrt(square - mean * mean + 1e-05)
    for j in range(cols):
        at = order_ref[j]
        part = (moved_ref[at].astype(F32) - mean) * scale * gain_ref[at, :1, :]
        part = part.astype(BF)
        first_ref[:, j * chans : (j + 1) * chans] = part[:half]
        second_ref[:, j * chans : (j + 1) * chans] = part[half:]


def normalize(order, moved, gains, half):
    cols, _, chans = moved.shape
    shape = jax.ShapeDtypeStruct((half, cols * chans), BF)
    return pl.pallas_call(
        act_kernel,
        in_specs=[pl.BlockSpec(memory_space=pltpu.SMEM)] + [pl.BlockSpec(memory_space=pltpu.VMEM)] * 2,
        out_shape=(shape, shape),
        compiler_params=params(16),
    )(order, moved, gains)


def mm1_kernel(count, block, *refs):
    pieces, weights, (b_ref, o_ref) = refs[:count], refs[count:-2], refs[-2:]
    total = None
    at = 0
    for w_ref in weights:
        size = w_ref.shape[0]
        left = jnp.concatenate([p[:, :, at : at + size].reshape(-1, size) for p in pieces], axis=0)
        term = jnp.dot(left, w_ref[...], preferred_element_type=F32)
        total = term if total is None else total + term
        at += size
    pre = total + b_ref[...]
    o_ref[...] = (0.5 * pre * (1.0 + lax.erf(pre * math.sqrt(0.5)))).astype(BF)


def matmul_in(pieces, weights, b):
    width = weights[0].shape[1]
    depth = pieces[0].shape[2]
    tokens = sum(p.shape[0] * p.shape[1] for p in pieces)
    tile = 256
    return pl.pallas_call(
        functools.partial(mm1_kernel, len(pieces), 768),
        grid=(width // tile,),
        in_specs=[pl.BlockSpec(p.shape, lambda i: (0, 0, 0)) for p in pieces]
        + [pl.BlockSpec((w.shape[0], tile), lambda i: (0, i)) for w in weights]
        + [pl.BlockSpec((1, tile), lambda i: (0, i))],
        out_specs=pl.BlockSpec((tokens, tile), lambda i: (0, i)),
        out_shape=jax.ShapeDtypeStruct((tokens, width), BF),
        compiler_params=params(62),
        cost_estimate=pl.CostEstimate(
            flops=2 * tokens * depth * width,
            bytes_accessed=2 * (tokens * depth + depth * width),
            transcendentals=0,
        ),
    )(*pieces, *weights, b[None])


def mm2_kernel(h_ref, w_ref, *outs):
    out = jnp.dot(h_ref[...], w_ref[0], preferred_element_type=F32)
    at = 0
    for o_ref in outs:
        rows = o_ref.shape[0] * o_ref.shape[1]
        o_ref[...] = out[at : at + rows].astype(BF).reshape(o_ref.shape)
        at += rows


def matmul_out(hidden, w, shapes):
    cols, depth, chans = w.shape
    tokens = hidden.shape[0]
    return pl.pallas_call(
        mm2_kernel,
        grid=(cols,),
        in_specs=[
            pl.BlockSpec((tokens, depth), lambda j: (0, 0)),
            pl.BlockSpec((1, depth, chans), lambda j: (j, 0, 0)),
        ],
        out_specs=[pl.BlockSpec(s[:2] + (chans,), lambda j: (0, 0, j)) for s in shapes],
        out_shape=[jax.ShapeDtypeStruct(s, BF) for s in shapes],
        compiler_params=params(62),
        cost_estimate=pl.CostEstimate(
            flops=2 * tokens * depth * cols * chans,
            bytes_accessed=2 * (tokens * depth + depth * cols * chans + tokens * cols * chans),
            transcendentals=0,
        ),
    )(hidden, w)


def merge_kernel(l1, r1, l2, r2, low1, top1, low2, top2, ol1, or1, ol2, or2):
    for a, b, o in ((l1, low1, ol1), (r1, top1, or1), (l2, low2, ol2), (r2, top2, or2)):
        o[...] = (a[...].astype(F32) + b[...].astype(F32)).astype(BF)


def merge(left1, right1, left2, right2, low1, top1, low2, top2):
    count, half, width = left1.shape
    tile = width // 4
    block = (count // 2, half, tile)
    low = pl.BlockSpec(block, lambda j: (1, 0, j))
    top = pl.BlockSpec(block, lambda j: (0, 0, j))
    return pl.pallas_call(
        merge_kernel,
        grid=(width // tile,),
        in_specs=[low, top, low, top, top, top, top, top],
        out_specs=[low, top, low, top],
        out_shape=[jax.ShapeDtypeStruct(left1.shape, BF)] * 4,
        input_output_aliases={0: 0, 1: 1, 2: 2, 3: 3},
        compiler_params=params(16),
    )(left1, right1, left2, right2, low1, top1, low2, top2)


def add_kernel(a, b, c, *outs):
    total = a[...].astype(F32) + (b[...].astype(F32) + c[...].astype(F32))
    for i, o_ref in enumerate(outs):
        o_ref[...] = total[i].astype(BF)


def add_pieces(parts):
    count, half, width = parts[0].shape
    tile = width // 4
    return pl.pallas_call(
        add_kernel,
        grid=(width // tile,),
        in_specs=[pl.BlockSpec((count, half, tile), lambda j: (0, 0, j))] * len(parts),
        out_specs=[pl.BlockSpec((half, tile), lambda j: (0, j))] * count,
        out_shape=[jax.ShapeDtypeStruct((half, width), BF)] * count,
        compiler_params=params(16),
    )(*parts)


def last_kernel(a, b, c, d, e, f, g, h, o_ref):
    half = a.shape[0]
    top = (a[...].astype(F32) + b[...].astype(F32)) + (c[...].astype(F32) + d[...].astype(F32))
    low = (e[...].astype(F32) + f[...].astype(F32)) + (g[...].astype(F32) + h[...].astype(F32))
    o_ref[0, :half, :] = top.astype(BF)
    o_ref[0, half:, :] = low.astype(BF)


def add_last(first, second, cols):
    half, width = first[0].shape
    chans = width // cols
    return pl.pallas_call(
        last_kernel,
        grid=(cols,),
        in_specs=[pl.BlockSpec((half, chans), lambda j: (0, j))] * 8,
        out_specs=pl.BlockSpec((1, 2 * half, chans), lambda j: (j, 0, 0)),
        out_shape=jax.ShapeDtypeStruct((cols, 2 * half, chans), BF),
        compiler_params=params(16),
    )(*first, *second)


def exchange(a, axis):
    return lax.all_to_all(a, axis, split_axis=0, concat_axis=0, tiled=True)


def tie_kernel(*refs):
    pass


def tie(values, others):
    count = len(values)
    anywhere = pl.BlockSpec(memory_space=pl.ANY)
    return pl.pallas_call(
        tie_kernel,
        in_specs=[anywhere] * (count + len(others)),
        out_specs=[anywhere] * count,
        out_shape=[jax.ShapeDtypeStruct(v.shape, v.dtype) for v in values],
        input_output_aliases={i: i for i in range(count)},
        compiler_params=params(62),
    )(*values, *others)


def spectral(image, filter_bank, gain_first, early, late):
    rows_here, width, chans = image.shape
    groups = lax.axis_size("row")
    width_all = chans * lax.axis_size("col")
    tokens = rows_here * width
    one, two, three, four = spectral_tables(rows_here, width, rows_here * groups)
    high = lax.Precision.HIGH
    source = image.astype(F32).reshape(tokens, chans)
    sums, squares = lax.psum(
        (jnp.sum(source, axis=-1), jnp.sum(source * source, axis=-1)), "col"
    )
    mean = sums[:, None] / width_all
    square = squares[:, None] / width_all
    normed = (source - mean) / jnp.sqrt(square - mean * mean + 1e-05) * gain_first
    col = jnp.dot(one, normed, precision=high).astype(BF)
    col = exchange(col.reshape(groups, -1, chans), "row").reshape(-1, chans)
    col, *early = tie([col, *early], [])
    spec = jnp.dot(two, col.astype(F32), precision=high)
    split = spec.shape[0] // 2
    spec_re, spec_im = spec[:split], spec[split:]
    f_re, f_im = filter_bank[0].reshape(-1, chans), filter_bank[1].reshape(-1, chans)
    filt = jnp.concatenate(
        [f_re * spec_re - f_im * spec_im, f_re * spec_im + f_im * spec_re], axis=0
    )
    back = jnp.dot(three, filt, precision=high).astype(BF)
    back = exchange(back.reshape(groups, -1, chans), "row").reshape(-1, chans)
    back, *late = tie([back, *late], [])
    return source + jnp.dot(four, back.astype(F32), precision=high), early, late


def weight_order():
    table = []
    for x in range(SIDE):
        for core in range(2):
            steps = [((x + dx) % SIDE, core ^ other) for dx in (0, -1, 1, 2) for other in (0, 1)]
            table.append([2 * at + c for at, c in steps])
    return jnp.asarray(np.array(table, np.int32))[lax.axis_index("col")]


def gather_near(a, axis):
    return jnp.stack([a] + [along(a, axis, s) for s in (1, -1, 2)])


def gather_far(a, axis, waits):
    half = a.shape[0] // 2
    left, right = along(a, axis, 1), along(a, axis, -1)
    left, right = tie([left, right], waits)
    return [a, left, right, along(left[:half], axis, 1), along(right[half:], axis, -1)]


def send_back(parts, axis):
    return [parts[0]] + [along(p, axis, s) for p, s in zip(parts[1:], (-1, 1, 2))]


def on_device(image, filter_bank, gain_first, gain_second, w_in, b_in, w_out, b_out):
    rows_here, width, chans = image.shape
    cols = lax.axis_size("col")
    padded = jnp.pad(gain_second[None], ((0, 63), (0, 0)))
    gains = lax.all_gather(padded, "col", axis=0, tiled=False)
    swap = functools.partial(shift_col, dx=0, dc=1)
    w_half = w_in.shape[0] // 2
    sibling = swap(w_in)
    ends = [w_in[:w_half], w_in[w_half:]]
    early, late = [[shift_col(end, 1, 0), shift_col(end, -1, 0)] for end in ends]
    w_out_all = lax.all_gather(w_out, "col", axis=0, tiled=False)
    resid, (up0, down0, sibling), (up1, down1) = spectral(
        image, filter_bank, gain_first, early + [sibling], late
    )
    near = [up0, up1, down0, down1]
    near_swap = [swap(part) for part in near]
    far = [shift_col(up0, 1, 0), shift_col(down1, -1, 0)]
    far_swap = [swap(part) for part in far]
    weights = [w_in, sibling] + near[:2] + near_swap[:2] + near[2:] + near_swap[2:] + far + far_swap
    tokens = rows_here * width
    own = tokens // cols
    half = own // 2
    moved = exchange(resid.astype(BF).reshape(cols, own, chans), "col")
    (moved,) = tie([moved], near_swap)
    first, second = normalize(weight_order(), moved, gains, half)
    first, second = gather_near(first, "z"), gather_near(second, "y")
    first, second = tie([first, second], far)
    pieces = gather_far(first, "y", far_swap) + gather_far(second, "z", far_swap)
    hidden = matmul_in(pieces, weights, b_in)
    outs = matmul_out(hidden, w_out_all, [p.shape for p in pieces])
    own1, left1, right1, top1, low1, own2, left2, right2, top2, low2 = outs
    left1, right1, left2, right2 = merge(
        left1,
        right1,
        left2,
        right2,
        along(low1, "y", -1),
        along(top1, "y", 1),
        along(low2, "z", -1),
        along(top2, "z", 1),
    )
    first = add_pieces([own1, along(right1, "y", 1), along(left1, "y", -1)])
    second = add_pieces([own2, along(right2, "z", 1), along(left2, "z", -1)])
    proj = exchange(add_last(send_back(first, "z"), send_back(second, "y"), cols), "col")
    result = (resid + proj.reshape(tokens, chans).astype(F32) + b_out).astype(BF)
    return result.reshape(rows_here, width, chans)


def solution(mesh):
    placed = (
        P("row", None, "col"),
        P(None, None, "row", "col"),
        P("col"),
        P("col"),
        P("col", "row"),
        P("row"),
        P("row", "col"),
        P("col"),
    )
    return jax.shard_map(
        on_device, mesh=mesh, in_specs=placed, out_specs=P("row", None, "col"), check_vma=False
    )
```

```python
import functools
import math

import jax
import jax.numpy as jnp
import numpy as np
from jax import lax
from jax.experimental import pallas as pl
from jax.experimental.pallas import tpu as pltpu
from jax.sharding import PartitionSpec as P

SIDE = 4
BF = jnp.bfloat16
F32 = jnp.float32
MB = 1 << 20


def angles(count):
    index = np.arange(count)
    turn = (index[:, None] * index[None, :]) % count * (2.0 * math.pi / count)
    return np.cos(turn), np.sin(turn)


def spectral_tables(here, width, height):
    groups = height // here
    per = width // groups
    cos_w, sin_w = angles(width)
    cos_h, sin_h = angles(height)
    eye_r, eye_k = np.eye(here), np.eye(per)
    out = np.stack([cos_w, -sin_w]).reshape(2, width, groups, per)
    one = np.einsum("scqk,rt->qrsktc", out, eye_r).reshape(2 * here * width, here * width)
    turn = np.stack([np.stack([cos_h, sin_h]), np.stack([-sin_h, cos_h])])
    turn = turn.reshape(2, 2, groups, here, height)
    two = np.einsum("uvqrn,kl->unkqrvl", turn, eye_k).reshape(2 * height * per, 2 * height * per)
    back = np.stack([np.stack([cos_h, -sin_h]), np.stack([sin_h, cos_h])])
    back = back.reshape(2, 2, height, groups, here)
    three = np.einsum("uvnqr,kl->qrukvnl", back, eye_k).reshape(2 * height * per, 2 * height * per)
    four = np.einsum("sqkc,rt->rcqtsk", out.transpose(0, 2, 3, 1), eye_r)
    four = four.reshape(here * width, 2 * here * width) / (width * height)
    return [t.astype(np.float32) for t in (one, two, three, four)]


def hop(a, axis, steps):
    pairs = []
    for z in range(SIDE):
        for y in range(SIDE):
            for x in range(SIDE):
                for core, step in enumerate(steps):
                    to = {"z": z, "y": y, "x": x}
                    to[axis] = (to[axis] + step) % SIDE
                    source = ((z * SIDE + y) * SIDE + x) * 2 + core
                    pairs.append((source, ((to["z"] * SIDE + to["y"]) * SIDE + to["x"]) * 2 + core))
    return lax.ppermute(a, ("row", "col"), pairs)


APART = (1, -1)
OTHER = (-1, 1)


def swap_cores(a):
    pairs = [(x * 2 + core, x * 2 + 1 - core) for x in range(SIDE) for core in range(2)]
    return lax.ppermute(a, "col", pairs)


def params(mb):
    return pltpu.CompilerParams(vmem_limit_bytes=mb * MB)


def act_kernel(moved_ref, gain_ref, first_ref, second_ref):
    cols, _, chans = moved_ref.shape
    half = first_ref.shape[0]
    values = moved_ref[...].astype(F32)
    mean = jnp.sum(jnp.sum(values, axis=0), axis=-1, keepdims=True) / (cols * chans)
    square = jnp.sum(jnp.sum(values * values, axis=0), axis=-1, keepdims=True) / (cols * chans)
    scale = 1.0 / jnp.sqrt(square - mean * mean + 1e-05)
    for j in range(cols):
        part = (values[j] - mean) * scale * gain_ref[j, :1, :]
        part = part.astype(BF)
        first_ref[:, j * chans : (j + 1) * chans] = part[:half]
        second_ref[:, j * chans : (j + 1) * chans] = part[half:]


def normalize(moved, gains, half):
    cols, _, chans = moved.shape
    shape = jax.ShapeDtypeStruct((half, cols * chans), BF)
    return pl.pallas_call(
        act_kernel,
        out_shape=(shape, shape),
        compiler_params=params(63),
    )(moved, gains)


def mm1_kernel(*refs):
    pieces, (w_ref, b_ref, o_ref, left, sems) = refs[:-5], refs[-5:]
    rows = left.shape[0] // len(pieces)
    copies = [
        pltpu.make_async_copy(p, left.at[pl.ds(i * rows, rows)], sems.at[i])
        for i, p in enumerate(pieces)
    ]

    @pl.when(pl.program_id(0) == 0)
    def _():
        for copy in copies:
            copy.start()
        for copy in copies:
            copy.wait()

    pre = jnp.dot(left[...], w_ref[...], preferred_element_type=F32) + b_ref[...]
    o_ref[...] = (0.5 * pre * (1.0 + lax.erf(pre * math.sqrt(0.5)))).astype(BF)


def matmul_in(pieces, w, b):
    depth, width = w.shape
    tokens = len(pieces) * pieces[0].shape[0]
    tile = 256
    return pl.pallas_call(
        mm1_kernel,
        grid=(width // tile,),
        in_specs=[pl.BlockSpec(memory_space=pl.ANY) for _ in pieces]
        + [
            pl.BlockSpec((depth, tile), lambda i: (0, i)),
            pl.BlockSpec((1, tile), lambda i: (0, i)),
        ],
        out_specs=pl.BlockSpec((tokens, tile), lambda i: (0, i)),
        out_shape=jax.ShapeDtypeStruct((tokens, width), BF),
        scratch_shapes=[pltpu.VMEM((tokens, depth), BF), pltpu.SemaphoreType.DMA((len(pieces),))],
        compiler_params=params(63),
        cost_estimate=pl.CostEstimate(
            flops=2 * tokens * depth * width,
            bytes_accessed=2 * (tokens * depth + depth * width),
            transcendentals=0,
        ),
    )(*pieces, w, b[None])


def mm2_kernel(count, *refs):
    h_ref, weights, outs, (held, sems) = refs[0], refs[1 : 1 + count], refs[1 + count : -2], refs[-2:]
    step = pl.program_id(0)
    copies = [pltpu.make_async_copy(w, held.at[j % 2], sems.at[j % 2]) for j, w in enumerate(weights)]
    for j in range(count):

        @pl.when(step == j)
        def _(j=j):
            if j == 0:
                copies[0].start()
            if j + 1 < count:
                copies[j + 1].start()
            copies[j].wait()

    out = jnp.dot(h_ref[...], held[lax.rem(step, 2)], preferred_element_type=F32)
    rows = outs[0].shape[0]
    for i, o_ref in enumerate(outs):
        o_ref[...] = out[i * rows : (i + 1) * rows].astype(BF)


def matmul_out(hidden, weights, count):
    depth, chans = weights[0].shape
    tokens = hidden.shape[0]
    cols = len(weights)
    rows = tokens // count
    return pl.pallas_call(
        functools.partial(mm2_kernel, cols),
        grid=(cols,),
        in_specs=[pl.BlockSpec((tokens, depth), lambda j: (0, 0))]
        + [pl.BlockSpec(memory_space=pl.ANY) for _ in weights],
        out_specs=[pl.BlockSpec((rows, chans), lambda j: (0, j))] * count,
        out_shape=[jax.ShapeDtypeStruct((rows, cols * chans), BF)] * count,
        scratch_shapes=[pltpu.VMEM((2, depth, chans), BF), pltpu.SemaphoreType.DMA((2,))],
        compiler_params=params(63),
        cost_estimate=pl.CostEstimate(
            flops=2 * tokens * depth * cols * chans,
            bytes_accessed=2 * (tokens * depth + depth * cols * chans + tokens * cols * chans),
            transcendentals=0,
        ),
    )(hidden, *weights)


def pair_kernel(a1, b1, a2, b2, o1, o2):
    o1[...] = (a1[...].astype(F32) + b1[...].astype(F32)).astype(BF)
    o2[...] = (a2[...].astype(F32) + b2[...].astype(F32)).astype(BF)


def add_pairs(*parts):
    rows, width = parts[0].shape
    tile = width // 4
    block = pl.BlockSpec((rows, tile), lambda j: (0, j))
    return pl.pallas_call(
        pair_kernel,
        grid=(width // tile,),
        in_specs=[block] * 4,
        out_specs=[block] * 2,
        out_shape=[jax.ShapeDtypeStruct((rows, width), BF)] * 2,
        compiler_params=params(63),
    )(*parts)


def add_kernel(a, b, c, *outs):
    total = a[...].astype(F32) + (b[...].astype(F32) + c[...].astype(F32))
    rows = outs[0].shape[0]
    for i, o_ref in enumerate(outs):
        o_ref[...] = total[i * rows : (i + 1) * rows].astype(BF)


def add_pieces(*parts):
    rows, width = parts[0].shape
    tile = width // 4
    return pl.pallas_call(
        add_kernel,
        grid=(width // tile,),
        in_specs=[pl.BlockSpec((rows, tile), lambda j: (0, j))] * len(parts),
        out_specs=[pl.BlockSpec((rows // SIDE, tile), lambda j: (0, j))] * SIDE,
        out_shape=[jax.ShapeDtypeStruct((rows // SIDE, width), BF)] * SIDE,
        compiler_params=params(63),
    )(*parts)


def last_kernel(place_ref, a, b, c, d, e, f, g, h, o_ref):
    half = a.shape[0]
    top = (a[...].astype(F32) + b[...].astype(F32)) + (c[...].astype(F32) + d[...].astype(F32))
    low = (e[...].astype(F32) + f[...].astype(F32)) + (g[...].astype(F32) + h[...].astype(F32))
    o_ref[0, :half, :] = top.astype(BF)
    o_ref[0, half:, :] = low.astype(BF)


def add_last(place, first, second, cols):
    half, width = first[0].shape
    chans = width // cols
    return pl.pallas_call(
        last_kernel,
        grid_spec=pltpu.PrefetchScalarGridSpec(
            num_scalar_prefetch=1,
            grid=(cols,),
            in_specs=[pl.BlockSpec((half, chans), lambda j, place: (0, j))] * 8,
            out_specs=pl.BlockSpec((1, 2 * half, chans), lambda j, place: (place[j], 0, 0)),
        ),
        out_shape=jax.ShapeDtypeStruct((cols, 2 * half, chans), BF),
        compiler_params=params(63),
    )(place, *first, *second)


def exchange(a, axis):
    return lax.all_to_all(a, axis, split_axis=0, concat_axis=0, tiled=True)


def tie_kernel(*refs):
    pass


def tie(values, others):
    count = len(values)
    anywhere = pl.BlockSpec(memory_space=pl.ANY)
    return pl.pallas_call(
        tie_kernel,
        in_specs=[anywhere] * (count + len(others)),
        out_specs=[anywhere] * count,
        out_shape=[jax.ShapeDtypeStruct(v.shape, v.dtype) for v in values],
        input_output_aliases={i: i for i in range(count)},
        compiler_params=params(62),
    )(*values, *others)


def spectral(image, filter_bank, gain_first, late):
    rows_here, width, chans = image.shape
    groups = lax.axis_size("row")
    width_all = chans * lax.axis_size("col")
    tokens = rows_here * width
    one, two, three, four = spectral_tables(rows_here, width, rows_here * groups)
    high = lax.Precision.HIGH
    source = image.astype(F32).reshape(tokens, chans)
    sums, squares = lax.psum(
        (jnp.sum(source, axis=-1), jnp.sum(source * source, axis=-1)), "col"
    )
    mean = sums[:, None] / width_all
    square = squares[:, None] / width_all
    normed = (source - mean) / jnp.sqrt(square - mean * mean + 1e-05) * gain_first
    col = jnp.dot(one, normed, precision=high).astype(BF)
    col = exchange(col.reshape(groups, -1, chans), "row").reshape(-1, chans)
    spec = jnp.dot(two, col.astype(F32), precision=high)
    split = spec.shape[0] // 2
    spec_re, spec_im = spec[:split], spec[split:]
    f_re, f_im = filter_bank[0].reshape(-1, chans), filter_bank[1].reshape(-1, chans)
    filt = jnp.concatenate(
        [f_re * spec_re - f_im * spec_im, f_re * spec_im + f_im * spec_re], axis=0
    )
    back = jnp.dot(three, filt, precision=high).astype(BF)
    back = exchange(back.reshape(groups, -1, chans), "row").reshape(-1, chans)
    back, *late = tie([back, *late], [])
    return source + jnp.dot(four, back.astype(F32), precision=high), late


def block_places():
    table = []
    for x in range(SIDE):
        for core in range(2):
            row = []
            for far in (False, True):
                at = core ^ far
                for step in (0, APART[at], OTHER[at], 2):
                    row.append((x + (step if step == 0 else -step)) % SIDE * 2 + at)
            table.append(row)
    return jnp.asarray(np.array(table, np.int32))[lax.axis_index("col")]


def gather_near(a, axis):
    far, *near = [hop(a, axis, (s, s)) for s in (2, 1, -1)]
    return jnp.stack([a, *near, far]).reshape(-1, a.shape[1])


def send_back(parts, axis):
    far, *near = [hop(parts[i], axis, (s, s)) for i, s in ((3, 2), (1, -1), (2, 1))]
    return [parts[0], *near, far]


def on_device(image, filter_bank, gain_first, gain_second, w_in, b_in, w_out, b_out):
    rows_here, width, chans = image.shape
    cols = lax.axis_size("col")
    padded = jnp.pad(gain_second[None], ((0, 63), (0, 0)))
    w_in_all = lax.all_gather(w_in, "col", axis=0, tiled=True)
    gains = lax.all_gather(padded, "col", axis=0, tiled=False)
    one = hop(w_out, "x", APART)
    own_swap = swap_cores(w_out)
    resid, (one, own_swap) = spectral(image, filter_bank, gain_first, [one, own_swap])
    one_swap = swap_cores(one)
    tokens = rows_here * width
    own = tokens // cols
    half = own // 2
    moved = exchange(resid.astype(BF).reshape(cols, own, chans), "col")
    moved, one, one_swap, later = tie([moved, one, one_swap, w_out], [])
    first, second = normalize(moved, gains, half)
    first, second = gather_near(first, "z"), gather_near(second, "y")
    first, second, later = tie([first, second, later], [])
    two = hop(later, "x", OTHER)
    first = [first, hop(first, "y", APART), hop(first, "y", OTHER)]
    second = [second, hop(second, "z", APART), hop(second, "z", OTHER)]
    first[1], second[1], one = tie([first[1], second[1], one], [])
    three = hop(one, "x", APART)
    first.append(hop(first[1], "y", APART))
    second.append(hop(second[1], "z", APART))
    *pieces, two = tie(first + second + [two], [])
    two_swap = swap_cores(two)
    hidden = matmul_in(pieces, w_in_all, b_in)
    hidden, three = tie([hidden, three], [])
    blocks = [later, one, two, three, own_swap, one_swap, two_swap, swap_cores(three)]
    own1, fore1, back1, far1, own2, fore2, back2, far2 = matmul_out(hidden, blocks, len(pieces))
    back1, back2 = hop(back1, "y", APART), hop(back2, "z", APART)
    fore1, fore2 = add_pairs(fore1, hop(far1, "y", OTHER), fore2, hop(far2, "z", OTHER))
    first = add_pieces(own1, back1, hop(fore1, "y", OTHER))
    second = add_pieces(own2, back2, hop(fore2, "z", OTHER))
    first, second = send_back(first, "z"), send_back(second, "y")
    proj = exchange(add_last(block_places(), first, second, cols), "col")
    result = (resid + proj.reshape(tokens, chans).astype(F32) + b_out).astype(BF)
    return result.reshape(rows_here, width, chans)


def solution(mesh):
    placed = (
        P("row", None, "col"),
        P(None, None, "row", "col"),
        P("col"),
        P("col"),
        P("col", "row"),
        P("row"),
        P("row", "col"),
        P("col"),
    )
    return jax.shard_map(
        on_device, mesh=mesh, in_specs=placed, out_specs=P("row", None, "col"), check_vma=False
    )
```

```python
import functools
import math

import jax
import jax.numpy as jnp
import numpy as np
from jax import lax
from jax.experimental import pallas as pl
from jax.experimental.pallas import tpu as pltpu
from jax.sharding import PartitionSpec as P

SIDE = 4
BF = jnp.bfloat16
F32 = jnp.float32
MB = 1 << 20


def angles(count):
    index = np.arange(count)
    turn = (index[:, None] * index[None, :]) % count * (2.0 * math.pi / count)
    return np.cos(turn), np.sin(turn)


def spectral_tables(here, width, height):
    groups = height // here
    per = width // groups
    cos_w, sin_w = angles(width)
    cos_h, sin_h = angles(height)
    eye_r, eye_k = np.eye(here), np.eye(per)
    out = np.stack([cos_w, -sin_w]).reshape(2, width, groups, per)
    one = np.einsum("scqk,rt->qrsktc", out, eye_r).reshape(2 * here * width, here * width)
    turn = np.stack([np.stack([cos_h, sin_h]), np.stack([-sin_h, cos_h])])
    turn = turn.reshape(2, 2, groups, here, height)
    two = np.einsum("uvqrn,kl->unkqrvl", turn, eye_k).reshape(2 * height * per, 2 * height * per)
    back = np.stack([np.stack([cos_h, -sin_h]), np.stack([sin_h, cos_h])])
    back = back.reshape(2, 2, height, groups, here)
    three = np.einsum("uvnqr,kl->qrukvnl", back, eye_k).reshape(2 * height * per, 2 * height * per)
    four = np.einsum("sqkc,rt->rcqtsk", out.transpose(0, 2, 3, 1), eye_r)
    four = four.reshape(here * width, 2 * here * width) / (width * height)
    return [t.astype(np.float32) for t in (one, two, three, four)]


def hop(a, axis, steps):
    pairs = []
    for z in range(SIDE):
        for y in range(SIDE):
            for x in range(SIDE):
                for core, step in enumerate(steps):
                    to = {"z": z, "y": y, "x": x}
                    to[axis] = (to[axis] + step) % SIDE
                    source = ((z * SIDE + y) * SIDE + x) * 2 + core
                    pairs.append((source, ((to["z"] * SIDE + to["y"]) * SIDE + to["x"]) * 2 + core))
    return lax.ppermute(a, ("row", "col"), pairs)


APART = (1, -1)
OTHER = (-1, 1)


def swap_cores(a):
    pairs = [(x * 2 + core, x * 2 + 1 - core) for x in range(SIDE) for core in range(2)]
    return lax.ppermute(a, "col", pairs)


def params(mb):
    return pltpu.CompilerParams(vmem_limit_bytes=mb * MB)


def act_kernel(moved_ref, first_ref, second_ref):
    cols, _, chans = moved_ref.shape
    half = first_ref.shape[0]
    values = moved_ref[:, : 2 * half, :].astype(F32)
    gains = jnp.sum(moved_ref[:, 2 * half :, :].astype(F32)[:, :3], axis=1)
    mean = jnp.sum(jnp.sum(values, axis=0), axis=-1, keepdims=True) / (cols * chans)
    square = jnp.sum(jnp.sum(values * values, axis=0), axis=-1, keepdims=True) / (cols * chans)
    scale = 1.0 / jnp.sqrt(square - mean * mean + 1e-05)
    for j in range(cols):
        part = ((values[j] - mean) * scale * gains[j][None, :]).astype(BF)
        first_ref[:, j * chans : (j + 1) * chans] = part[:half]
        second_ref[:, j * chans : (j + 1) * chans] = part[half:]


def normalize(moved, half):
    cols, _, chans = moved.shape
    shape = jax.ShapeDtypeStruct((half, cols * chans), BF)
    return pl.pallas_call(act_kernel, out_shape=(shape, shape), compiler_params=params(16))(moved)


def mm1_kernel(*refs):
    pieces, (w_ref, b_ref, o_ref, left, sems) = refs[:-5], refs[-5:]
    rows = left.shape[0] // len(pieces)
    copies = [
        pltpu.make_async_copy(p, left.at[pl.ds(i * rows, rows)], sems.at[i])
        for i, p in enumerate(pieces)
    ]

    @pl.when(pl.program_id(0) == 0)
    def _():
        for copy in copies:
            copy.start()
        for copy in copies:
            copy.wait()

    pre = jnp.dot(left[...], w_ref[...], preferred_element_type=F32) + b_ref[...]
    o_ref[...] = (0.5 * pre * (1.0 + lax.erf(pre * math.sqrt(0.5)))).astype(BF)


def matmul_in(pieces, w, b):
    depth, width = w.shape
    tokens = len(pieces) * pieces[0].shape[0]
    tile = 256
    return pl.pallas_call(
        mm1_kernel,
        grid=(width // tile,),
        in_specs=[pl.BlockSpec(memory_space=pl.ANY) for _ in pieces]
        + [
            pl.BlockSpec((depth, tile), lambda i: (0, i)),
            pl.BlockSpec((1, tile), lambda i: (0, i)),
        ],
        out_specs=pl.BlockSpec((tokens, tile), lambda i: (0, i)),
        out_shape=jax.ShapeDtypeStruct((tokens, width), BF),
        scratch_shapes=[pltpu.VMEM((tokens, depth), BF), pltpu.SemaphoreType.DMA((len(pieces),))],
        compiler_params=params(40),
        cost_estimate=pl.CostEstimate(
            flops=2 * tokens * depth * width,
            bytes_accessed=2 * (tokens * depth + depth * width),
            transcendentals=0,
        ),
    )(*pieces, w, b[None])


def mm2_kernel(count, *refs):
    h_ref, weights, outs, (held, sems) = refs[0], refs[1 : 1 + count], refs[1 + count : -2], refs[-2:]
    step = pl.program_id(0)
    copies = [pltpu.make_async_copy(w, held.at[j % 2], sems.at[j % 2]) for j, w in enumerate(weights)]
    for j in range(count):

        @pl.when(step == j)
        def _(j=j):
            if j == 0:
                copies[0].start()
            if j + 1 < count:
                copies[j + 1].start()
            copies[j].wait()

    out = jnp.dot(h_ref[...], held[lax.rem(step, 2)], preferred_element_type=F32)
    rows = outs[0].shape[0]
    for i, o_ref in enumerate(outs):
        o_ref[...] = out[i * rows : (i + 1) * rows].astype(BF)


def matmul_out(hidden, weights, count):
    depth, chans = weights[0].shape
    tokens = hidden.shape[0]
    cols = len(weights)
    rows = tokens // count
    return pl.pallas_call(
        functools.partial(mm2_kernel, cols),
        grid=(cols,),
        in_specs=[pl.BlockSpec((tokens, depth), lambda j: (0, 0))]
        + [pl.BlockSpec(memory_space=pl.ANY) for _ in weights],
        out_specs=[pl.BlockSpec((rows, chans), lambda j: (0, j))] * count,
        out_shape=[jax.ShapeDtypeStruct((rows, cols * chans), BF)] * count,
        scratch_shapes=[pltpu.VMEM((2, depth, chans), BF), pltpu.SemaphoreType.DMA((2,))],
        compiler_params=params(40),
        cost_estimate=pl.CostEstimate(
            flops=2 * tokens * depth * cols * chans,
            bytes_accessed=2 * (tokens * depth + depth * cols * chans + tokens * cols * chans),
            transcendentals=0,
        ),
    )(hidden, *weights)


def pair_kernel(a1, b1, a2, b2, o1, o2):
    o1[...] = (a1[...].astype(F32) + b1[...].astype(F32)).astype(BF)
    o2[...] = (a2[...].astype(F32) + b2[...].astype(F32)).astype(BF)


def add_pairs(*parts):
    rows, width = parts[0].shape
    tile = width // 2
    block = pl.BlockSpec((rows, tile), lambda j: (0, j))
    return pl.pallas_call(
        pair_kernel,
        grid=(width // tile,),
        in_specs=[block] * 4,
        out_specs=[block] * 2,
        out_shape=[jax.ShapeDtypeStruct((rows, width), BF)] * 2,
        compiler_params=params(24),
    )(*parts)


def add_kernel(a, b, c, *outs):
    total = a[...].astype(F32) + (b[...].astype(F32) + c[...].astype(F32))
    rows = outs[0].shape[0]
    for i, o_ref in enumerate(outs):
        o_ref[...] = total[i * rows : (i + 1) * rows].astype(BF)


def add_pieces(*parts):
    rows, width = parts[0].shape
    tile = width // 2
    return pl.pallas_call(
        add_kernel,
        grid=(width // tile,),
        in_specs=[pl.BlockSpec((rows, tile), lambda j: (0, j))] * len(parts),
        out_specs=[pl.BlockSpec((rows // SIDE, tile), lambda j: (0, j))] * SIDE,
        out_shape=[jax.ShapeDtypeStruct((rows // SIDE, width), BF)] * SIDE,
        compiler_params=params(24),
    )(*parts)


def last_kernel(place_ref, a, b, c, d, e, f, g, h, o_ref):
    half = a.shape[0]
    cols, _, chans = o_ref.shape
    for j in range(cols):
        at = pl.ds(j * chans, chans)
        top, low = [
            sum(p[:, at].astype(F32) for p in parts).astype(BF)
            for parts in ((a, b, c, d), (e, f, g, h))
        ]
        o_ref[place_ref[j], :half, :] = top
        o_ref[place_ref[j], half:, :] = low


def add_last(place, first, second, cols):
    half, width = first[0].shape
    return pl.pallas_call(
        last_kernel,
        in_specs=[pl.BlockSpec(memory_space=pltpu.SMEM)] + [pl.BlockSpec(memory_space=pltpu.VMEM)] * 8,
        out_shape=jax.ShapeDtypeStruct((cols, 2 * half, width // cols), BF),
        compiler_params=params(16),
    )(place, *first, *second)


def exchange(a, axis):
    return lax.all_to_all(a, axis, split_axis=0, concat_axis=0, tiled=True)


def tie_kernel(*refs):
    pass


def tie(values, others):
    count = len(values)
    anywhere = pl.BlockSpec(memory_space=pl.ANY)
    return pl.pallas_call(
        tie_kernel,
        in_specs=[anywhere] * (count + len(others)),
        out_specs=[anywhere] * count,
        out_shape=[jax.ShapeDtypeStruct(v.shape, v.dtype) for v in values],
        input_output_aliases={i: i for i in range(count)},
        compiler_params=params(1),
    )(*values, *others)


def spectral(image, filter_bank, gain_first):
    rows_here, width, chans = image.shape
    groups = lax.axis_size("row")
    width_all = chans * lax.axis_size("col")
    tokens = rows_here * width
    one, two, three, four = spectral_tables(rows_here, width, rows_here * groups)
    high = lax.Precision.HIGH
    source = image.astype(F32).reshape(tokens, chans)
    sums, squares = lax.psum(
        (jnp.sum(source, axis=-1), jnp.sum(source * source, axis=-1)), "col"
    )
    mean = sums[:, None] / width_all
    square = squares[:, None] / width_all
    normed = (source - mean) / jnp.sqrt(square - mean * mean + 1e-05) * gain_first
    col = jnp.dot(one, normed, precision=high).astype(BF)
    col = exchange(col.reshape(groups, -1, chans), "row").reshape(-1, chans)
    spec = jnp.dot(two, col.astype(F32), precision=high)
    split = spec.shape[0] // 2
    spec_re, spec_im = spec[:split], spec[split:]
    f_re, f_im = filter_bank[0].reshape(-1, chans), filter_bank[1].reshape(-1, chans)
    filt = jnp.concatenate(
        [f_re * spec_re - f_im * spec_im, f_re * spec_im + f_im * spec_re], axis=0
    )
    back = jnp.dot(three, filt, precision=high).astype(BF)
    back = exchange(back.reshape(groups, -1, chans), "row").reshape(-1, chans)
    return source + jnp.dot(four, back.astype(F32), precision=high)


def three_parts(gain):
    top = lax.reduce_precision(gain, 8, 7)
    mid = lax.reduce_precision(gain - top, 8, 7)
    return jnp.stack([top, mid, gain - top - mid]).astype(BF)


def block_places():
    table = []
    for x in range(SIDE):
        for core in range(2):
            row = []
            for far in (False, True):
                at = core ^ far
                for step in (0, APART[at], OTHER[at], 2):
                    row.append((x + (step if step == 0 else -step)) % SIDE * 2 + at)
            table.append(row)
    return jnp.asarray(np.array(table, np.int32))[lax.axis_index("col")]


def gather_near(a, axis):
    far, *near = [hop(a, axis, (s, s)) for s in (2, 1, -1)]
    return jnp.stack([a, *near, far]).reshape(-1, a.shape[1])


def send_back(parts, axis):
    far, *near = [hop(parts[i], axis, (s, s)) for i, s in ((3, 2), (1, -1), (2, 1))]
    return [parts[0], *near, far]


def on_device(image, filter_bank, gain_first, gain_second, w_in, b_in, w_out, b_out):
    rows_here, width, chans = image.shape
    cols = lax.axis_size("col")
    w_in_all = lax.all_gather(w_in, "col", axis=0, tiled=True)
    resid = spectral(image, filter_bank, gain_first)
    tokens = rows_here * width
    own = tokens // cols
    half = own // 2
    extra = jnp.pad(three_parts(gain_second), ((0, half - 3), (0, 0)))
    message = jnp.concatenate(
        [
            resid.astype(BF).reshape(cols, own, chans),
            jnp.broadcast_to(extra[None], (cols, half, chans)),
        ],
        axis=1,
    )
    moved = exchange(message, "col")
    moved, later = tie([moved, w_out], [])
    one = hop(later, "x", APART)
    first, second = normalize(moved, half)
    first, second = gather_near(first, "z"), gather_near(second, "y")
    first, second, later = tie([first, second, later], [])
    two = hop(later, "x", OTHER)
    first = [first, hop(first, "y", APART), hop(first, "y", OTHER)]
    second = [second, hop(second, "z", APART), hop(second, "z", OTHER)]
    first[1], second[1], one = tie([first[1], second[1], one], [])
    three = hop(one, "x", APART)
    first.append(hop(first[1], "y", APART))
    second.append(hop(second[1], "z", APART))
    *pieces, later, one, two = tie(first + second + [later, one, two], [])
    own_swap, one_swap, two_swap = swap_cores(later), swap_cores(one), swap_cores(two)
    hidden = matmul_in(pieces, w_in_all, b_in)
    hidden, three = tie([hidden, three], [])
    blocks = [later, one, two, three, own_swap, one_swap, two_swap, swap_cores(three)]
    own1, fore1, back1, far1, own2, fore2, back2, far2 = matmul_out(hidden, blocks, len(pieces))
    back1, back2 = hop(back1, "y", APART), hop(back2, "z", APART)
    fore1, fore2 = add_pairs(fore1, hop(far1, "y", OTHER), fore2, hop(far2, "z", OTHER))
    first = add_pieces(own1, back1, hop(fore1, "y", OTHER))
    second = add_pieces(own2, back2, hop(fore2, "z", OTHER))
    first, second = send_back(first, "z"), send_back(second, "y")
    proj = exchange(add_last(block_places(), first, second, cols), "col")
    result = (resid + proj.reshape(tokens, chans).astype(F32) + b_out).astype(BF)
    return result.reshape(rows_here, width, chans)


def solution(mesh):
    placed = (
        P("row", None, "col"),
        P(None, None, "row", "col"),
        P("col"),
        P("col"),
        P("col", "row"),
        P("row"),
        P("row", "col"),
        P("col"),
    )
    return jax.shard_map(
        on_device, mesh=mesh, in_specs=placed, out_specs=P("row", None, "col"), check_vma=False
    )
```

```python
import functools
import math

import jax
import jax.numpy as jnp
import numpy as np
from jax import lax
from jax.experimental import pallas as pl
from jax.experimental.pallas import tpu as pltpu
from jax.sharding import PartitionSpec as P

SIDE = 4
BF = jnp.bfloat16
F32 = jnp.float32
MB = 1 << 20


def angles(count):
    index = np.arange(count)
    turn = (index[:, None] * index[None, :]) % count * (2.0 * math.pi / count)
    return np.cos(turn), np.sin(turn)


def spectral_tables(here, width, height):
    groups = height // here
    per = width // groups
    cos_w, sin_w = angles(width)
    cos_h, sin_h = angles(height)
    eye_r, eye_k = np.eye(here), np.eye(per)
    out = np.stack([cos_w, -sin_w]).reshape(2, width, groups, per)
    one = np.einsum("scqk,rt->qrsktc", out, eye_r).reshape(2 * here * width, here * width)
    turn = np.stack([np.stack([cos_h, sin_h]), np.stack([-sin_h, cos_h])])
    turn = turn.reshape(2, 2, groups, here, height)
    two = np.einsum("uvqrn,kl->unkqrvl", turn, eye_k).reshape(2 * height * per, 2 * height * per)
    back = np.stack([np.stack([cos_h, -sin_h]), np.stack([sin_h, cos_h])])
    back = back.reshape(2, 2, height, groups, here)
    three = np.einsum("uvnqr,kl->qrukvnl", back, eye_k).reshape(2 * height * per, 2 * height * per)
    four = np.einsum("sqkc,rt->rcqtsk", out.transpose(0, 2, 3, 1), eye_r)
    four = four.reshape(here * width, 2 * here * width) / (width * height)
    return [t.astype(np.float32) for t in (one, two, three, four)]


def hop(a, axis, steps):
    pairs = []
    for z in range(SIDE):
        for y in range(SIDE):
            for x in range(SIDE):
                for core, step in enumerate(steps):
                    to = {"z": z, "y": y, "x": x}
                    to[axis] = (to[axis] + step) % SIDE
                    source = ((z * SIDE + y) * SIDE + x) * 2 + core
                    pairs.append((source, ((to["z"] * SIDE + to["y"]) * SIDE + to["x"]) * 2 + core))
    return lax.ppermute(a, ("row", "col"), pairs)


APART = (1, -1)
OTHER = (-1, 1)


def swap_cores(a):
    pairs = [(x * 2 + core, x * 2 + 1 - core) for x in range(SIDE) for core in range(2)]
    return lax.ppermute(a, "col", pairs)


def params(mb):
    return pltpu.CompilerParams(vmem_limit_bytes=mb * MB)


def act_kernel(moved_ref, first_ref, second_ref):
    cols, _, chans = moved_ref.shape
    half = first_ref.shape[0]
    values = moved_ref[:, : 2 * half, :].astype(F32)
    gains = jnp.sum(moved_ref[:, 2 * half :, :].astype(F32)[:, :3], axis=1)
    mean = jnp.sum(jnp.sum(values, axis=0), axis=-1, keepdims=True) / (cols * chans)
    square = jnp.sum(jnp.sum(values * values, axis=0), axis=-1, keepdims=True) / (cols * chans)
    scale = 1.0 / jnp.sqrt(square - mean * mean + 1e-05)
    for j in range(cols):
        part = ((values[j] - mean) * scale * gains[j][None, :]).astype(BF)
        first_ref[:, j * chans : (j + 1) * chans] = part[:half]
        second_ref[:, j * chans : (j + 1) * chans] = part[half:]


def normalize(moved, half):
    cols, _, chans = moved.shape
    shape = jax.ShapeDtypeStruct((half, cols * chans), BF)
    return pl.pallas_call(act_kernel, out_shape=(shape, shape), compiler_params=params(16))(moved)


def mm1_kernel(*refs):
    pieces, (w_ref, b_ref, o_ref) = refs[:-3], refs[-3:]
    left = jnp.concatenate([p[...] for p in pieces], axis=0)
    pre = jnp.dot(left, w_ref[...], preferred_element_type=F32) + b_ref[...]
    o_ref[...] = (0.5 * pre * (1.0 + lax.erf(pre * math.sqrt(0.5)))).astype(BF)


def matmul_in(pieces, w, b):
    depth, width = w.shape
    rows = pieces[0].shape[0]
    tokens = len(pieces) * rows
    tile = 256
    return pl.pallas_call(
        mm1_kernel,
        grid=(width // tile,),
        in_specs=[pl.BlockSpec((rows, depth), lambda i: (0, 0)) for _ in pieces]
        + [
            pl.BlockSpec((depth, tile), lambda i: (0, i)),
            pl.BlockSpec((1, tile), lambda i: (0, i)),
        ],
        out_specs=pl.BlockSpec((tokens, tile), lambda i: (0, i)),
        out_shape=jax.ShapeDtypeStruct((tokens, width), BF),
        compiler_params=params(58),
        cost_estimate=pl.CostEstimate(
            flops=2 * tokens * depth * width,
            bytes_accessed=2 * (tokens * depth + depth * width),
            transcendentals=0,
        ),
    )(*pieces, w, b[None])


def mm2_kernel(*refs):
    hiddens, (own_ref, other_ref), outs = refs[:SIDE], refs[SIDE : SIDE + 2], refs[SIDE + 2 :]
    rows, width = outs[0].shape
    chans = own_ref.shape[1]
    for i, h_ref in enumerate(hiddens):

        @pl.when(pl.program_id(0) == i)
        def _(h_ref=h_ref):
            for at, w_ref in ((0, own_ref), (chans, other_ref)):
                out = jnp.dot(h_ref[...], w_ref[...], preferred_element_type=F32)
                for p, o_ref in enumerate(outs):
                    o_ref[:, at : at + chans] = out[p * rows : (p + 1) * rows].astype(BF)


def matmul_out(hiddens, own, other, count):
    depth, chans = own.shape
    tokens = hiddens[0].shape[0]
    rows = tokens // count
    steps = len(hiddens)
    whole = pl.BlockSpec((depth, chans), lambda i: (0, 0))
    return pl.pallas_call(
        mm2_kernel,
        grid=(steps,),
        in_specs=[pl.BlockSpec((tokens, depth), lambda i: (0, 0))] * steps + [whole] * 2,
        out_specs=[pl.BlockSpec((rows, 2 * chans), lambda i: (i, 0))] * count,
        out_shape=[jax.ShapeDtypeStruct((steps * rows, 2 * chans), BF)] * count,
        compiler_params=params(58),
        cost_estimate=pl.CostEstimate(
            flops=4 * steps * tokens * depth * chans,
            bytes_accessed=2 * (steps * tokens * depth + 2 * depth * chans + 2 * steps * tokens * chans),
            transcendentals=0,
        ),
    )(*hiddens, own, other)


def pair_kernel(a, b, o):
    o[...] = (a[...].astype(F32) + b[...].astype(F32)).astype(BF)


def add_pair(a, b):
    rows, width = a.shape
    block = pl.BlockSpec((rows // 2, width), lambda j: (j, 0))
    return pl.pallas_call(
        pair_kernel,
        grid=(2,),
        in_specs=[block] * 2,
        out_specs=block,
        out_shape=jax.ShapeDtypeStruct((rows, width), BF),
        compiler_params=params(16),
    )(a, b)


def add_kernel(half, a, b, c, *outs):
    total = a[...].astype(F32) + (b[...].astype(F32) + c[...].astype(F32))
    for s, o_ref in enumerate(outs):
        for x in range(total.shape[0] // (SIDE * half)):
            at = (x * SIDE + s) * half
            o_ref[x * half : (x + 1) * half, :] = total[at : at + half].astype(BF)


def add_pieces(half, *parts):
    rows, width = parts[0].shape
    return pl.pallas_call(
        functools.partial(add_kernel, half),
        grid=(2,),
        in_specs=[pl.BlockSpec((rows // 2, width), lambda j: (j, 0))] * len(parts),
        out_specs=[pl.BlockSpec((rows // SIDE // 2, width), lambda j: (j, 0))] * SIDE,
        out_shape=[jax.ShapeDtypeStruct((rows // SIDE, width), BF)] * SIDE,
        compiler_params=params(24),
    )(*parts)


def sum_kernel(a, b, c, d, own_ref, other_ref):
    chans = own_ref.shape[1]
    total = (a[...].astype(F32) + b[...].astype(F32)) + (c[...].astype(F32) + d[...].astype(F32))
    own_ref[...] = total[:, :chans]
    other_ref[...] = total[:, chans:].astype(BF)


def add_last(parts):
    rows, width = parts[0].shape
    return pl.pallas_call(
        sum_kernel,
        out_shape=[
            jax.ShapeDtypeStruct((rows, width // 2), F32),
            jax.ShapeDtypeStruct((rows, width // 2), BF),
        ],
        compiler_params=params(16),
    )(*parts)


def finish_kernel(place_ref, own1, own2, got1, got2, resid_ref, bias_ref, o_ref):
    half = o_ref.shape[1] // 2
    for i in range(2 * SIDE):
        at = pl.ds(i % SIDE * half, half)
        for k, part in enumerate((own1, own2) if i < SIDE else (got1, got2)):
            to = pl.ds(k * half, half)
            value = part[at, :].astype(F32) + resid_ref[place_ref[i], to, :] + bias_ref[...]
            o_ref[place_ref[i], to, :] = value.astype(BF)


def finish(place, own1, own2, got1, got2, resid, bias):
    return pl.pallas_call(
        finish_kernel,
        in_specs=[pl.BlockSpec(memory_space=pltpu.SMEM)] + [pl.BlockSpec(memory_space=pltpu.VMEM)] * 6,
        out_shape=jax.ShapeDtypeStruct(resid.shape, BF),
        compiler_params=params(16),
    )(place, own1, own2, got1, got2, resid, bias[None])


def exchange(a, axis):
    return lax.all_to_all(a, axis, split_axis=0, concat_axis=0, tiled=True)


def tie_kernel(*refs):
    pass


def tie(values, others):
    count = len(values)
    anywhere = pl.BlockSpec(memory_space=pl.ANY)
    return pl.pallas_call(
        tie_kernel,
        in_specs=[anywhere] * (count + len(others)),
        out_specs=[anywhere] * count,
        out_shape=[jax.ShapeDtypeStruct(v.shape, v.dtype) for v in values],
        input_output_aliases={i: i for i in range(count)},
        compiler_params=params(62),
    )(*values, *others)


def spectral(image, filter_bank, gain_first):
    rows_here, width, chans = image.shape
    groups = lax.axis_size("row")
    width_all = chans * lax.axis_size("col")
    tokens = rows_here * width
    one, two, three, four = spectral_tables(rows_here, width, rows_here * groups)
    high = lax.Precision.HIGH
    source = image.astype(F32).reshape(tokens, chans)
    sums, squares = lax.psum(
        (jnp.sum(source, axis=-1), jnp.sum(source * source, axis=-1)), "col"
    )
    mean = sums[:, None] / width_all
    square = squares[:, None] / width_all
    normed = (source - mean) / jnp.sqrt(square - mean * mean + 1e-05) * gain_first
    col = jnp.dot(one, normed, precision=high).astype(BF)
    col = exchange(col.reshape(groups, -1, chans), "row").reshape(-1, chans)
    spec = jnp.dot(two, col.astype(F32), precision=high)
    split = spec.shape[0] // 2
    spec_re, spec_im = spec[:split], spec[split:]
    f_re, f_im = filter_bank[0].reshape(-1, chans), filter_bank[1].reshape(-1, chans)
    filt = jnp.concatenate(
        [f_re * spec_re - f_im * spec_im, f_re * spec_im + f_im * spec_re], axis=0
    )
    back = jnp.dot(three, filt, precision=high).astype(BF)
    back = exchange(back.reshape(groups, -1, chans), "row").reshape(-1, chans)
    return source + jnp.dot(four, back.astype(F32), precision=high)


def three_parts(gain):
    top = lax.reduce_precision(gain, 8, 7)
    mid = lax.reduce_precision(gain - top, 8, 7)
    return jnp.stack([top, mid, gain - top - mid]).astype(BF)


def block_places():
    table = []
    for x in range(SIDE):
        for core in range(2):
            row = []
            for far in (False, True):
                at = core ^ far
                for step in (0, APART[at], OTHER[at], 2):
                    row.append((x + (step if step == 0 else -step)) % SIDE * 2 + at)
            table.append(row)
    return jnp.asarray(np.array(table, np.int32))[lax.axis_index("col")]


def gather_near(a, axis):
    far, *near = [hop(a, axis, (s, s)) for s in (2, 1, -1)]
    return jnp.stack([a, *near, far]).reshape(-1, a.shape[1])


def gather_far(a, axis):
    one, two = hop(a, axis, APART), hop(a, axis, OTHER)
    return [a, one, two, hop(one, axis, APART)]


def reduce_far(outs, large, small, half):
    own, fore, back, far = outs
    far = hop(far, large, OTHER)
    back = hop(back, large, APART)
    fore = hop(add_pair(fore, far), large, OTHER)
    return send_back(add_pieces(half, own, back, fore), small)


def send_back(parts, axis):
    far, *near = [hop(parts[i], axis, (s, s)) for i, s in ((3, 2), (1, -1), (2, 1))]
    return [parts[0], *near, far]


def on_device(image, filter_bank, gain_first, gain_second, w_in, b_in, w_out, b_out):
    rows_here, width, chans = image.shape
    cols = lax.axis_size("col")
    w_in_all = lax.all_gather(w_in, "col", axis=0, tiled=True)
    resid = spectral(image, filter_bank, gain_first)
    tokens = rows_here * width
    own = tokens // cols
    half = own // 2
    extra = jnp.pad(three_parts(gain_second), ((0, half - 3), (0, 0)))
    message = jnp.concatenate(
        [
            resid.astype(BF).reshape(cols, own, chans),
            jnp.broadcast_to(extra[None], (cols, half, chans)),
        ],
        axis=1,
    )
    moved = exchange(message, "col")
    first, second = normalize(moved, half)
    first, second = gather_near(first, "z"), gather_near(second, "y")
    parts = [gather_far(first, "y"), gather_far(second, "z")]
    hiddens = [gather_far(matmul_in(part, w_in_all, b_in), "x") for part in parts]
    other = swap_cores(w_out)
    sums = []
    for hidden, (large, small) in zip(hiddens, (("y", "z"), ("z", "y"))):
        outs = matmul_out(hidden, w_out, other, SIDE)
        sums.append(add_last(reduce_far(outs, large, small, half)))
    (own1, give1), (own2, give2) = sums
    got1, got2 = swap_cores(give1), swap_cores(give2)
    resid = resid.reshape(cols, own, chans)
    result = finish(block_places(), own1, own2, got1, got2, resid, b_out)
    return result.reshape(rows_here, width, chans)


def solution(mesh):
    placed = (
        P("row", None, "col"),
        P(None, None, "row", "col"),
        P("col"),
        P("col"),
        P("col", "row"),
        P("row"),
        P("row", "col"),
        P("col"),
    )
    return jax.shard_map(
        on_device, mesh=mesh, in_specs=placed, out_specs=P("row", None, "col"), check_vma=False
    )
```

```python
import functools
import math

import jax
import jax.numpy as jnp
import numpy as np
from jax import lax
from jax.experimental import pallas as pl
from jax.experimental.pallas import tpu as pltpu
from jax.sharding import PartitionSpec as P

SIDE = 4
BF = jnp.bfloat16
F32 = jnp.float32
MB = 1 << 20


def angles(count):
    index = np.arange(count)
    turn = (index[:, None] * index[None, :]) % count * (2.0 * math.pi / count)
    return np.cos(turn), np.sin(turn)


def spectral_tables(here, width, height):
    groups = height // here
    per = width // groups
    cos_w, sin_w = angles(width)
    cos_h, sin_h = angles(height)
    eye_r, eye_k = np.eye(here), np.eye(per)
    out = np.stack([cos_w, -sin_w]).reshape(2, width, groups, per)
    one = np.einsum("scqk,rt->qrsktc", out, eye_r).reshape(2 * here * width, here * width)
    turn = np.stack([np.stack([cos_h, sin_h]), np.stack([-sin_h, cos_h])])
    turn = turn.reshape(2, 2, groups, here, height)
    two = np.einsum("uvqrn,kl->unkqrvl", turn, eye_k).reshape(2 * height * per, 2 * height * per)
    back = np.stack([np.stack([cos_h, -sin_h]), np.stack([sin_h, cos_h])])
    back = back.reshape(2, 2, height, groups, here)
    three = np.einsum("uvnqr,kl->qrukvnl", back, eye_k).reshape(2 * height * per, 2 * height * per)
    four = np.einsum("sqkc,rt->rcqtsk", out.transpose(0, 2, 3, 1), eye_r)
    four = four.reshape(here * width, 2 * here * width) / (width * height)
    return [t.astype(np.float32) for t in (one, two, three, four)]


def hop(a, axis, steps):
    pairs = []
    for z in range(SIDE):
        for y in range(SIDE):
            for x in range(SIDE):
                for core, step in enumerate(steps):
                    to = {"z": z, "y": y, "x": x}
                    to[axis] = (to[axis] + step) % SIDE
                    source = ((z * SIDE + y) * SIDE + x) * 2 + core
                    pairs.append((source, ((to["z"] * SIDE + to["y"]) * SIDE + to["x"]) * 2 + core))
    return lax.ppermute(a, ("row", "col"), pairs)


APART = (1, -1)
OTHER = (-1, 1)


def swap_cores(a):
    pairs = [(x * 2 + core, x * 2 + 1 - core) for x in range(SIDE) for core in range(2)]
    return lax.ppermute(a, "col", pairs)


def params(mb):
    return pltpu.CompilerParams(vmem_limit_bytes=mb * MB)


def act_kernel(cut, moved_ref, first_ref, second_ref):
    cols, _, chans = moved_ref.shape
    half = first_ref.shape[0]
    values = moved_ref[:, : 2 * half, :].astype(F32)
    gains = jnp.sum(moved_ref[:, 2 * half :, :].astype(F32)[:, :3], axis=1)
    mean = jnp.sum(jnp.sum(values, axis=0), axis=-1, keepdims=True) / (cols * chans)
    square = jnp.sum(jnp.sum(values * values, axis=0), axis=-1, keepdims=True) / (cols * chans)
    scale = 1.0 / jnp.sqrt(square - mean * mean + 1e-05)
    for j in range(cols):
        part = ((values[j] - mean) * scale * gains[j][None, :]).astype(BF)
        for low, high in ((0, cut), (cut, chans)):
            at = cols * low + j * (high - low)
            first_ref[:, at : at + high - low] = part[:half, low:high]
            second_ref[:, at : at + high - low] = part[half:, low:high]


def normalize(moved, half, cut):
    cols, _, chans = moved.shape
    shape = jax.ShapeDtypeStruct((half, cols * chans), BF)
    return pl.pallas_call(
        functools.partial(act_kernel, cut), out_shape=(shape, shape), compiler_params=params(16)
    )(moved)


def fill(sources, target, sems):
    rows = target.shape[0] // len(sources)
    copies = [
        pltpu.make_async_copy(source, target.at[pl.ds(i * rows, rows)], sems.at[i])
        for i, source in enumerate(sources)
    ]

    @pl.when(pl.program_id(0) == 0)
    def _():
        for copy in copies:
            copy.start()
        for copy in copies:
            copy.wait()


def mm1_kernel(*refs):
    pieces, (wa_ref, wb_ref, b_ref, o1_ref, o2_ref, left, sems) = refs[:-7], refs[-7:]
    fill(pieces, left, sems)
    cut = wa_ref.shape[0]
    pre = jnp.dot(left[:, :cut], wa_ref[...], preferred_element_type=F32)
    pre = pre + jnp.dot(left[:, cut:], wb_ref[...], preferred_element_type=F32) + b_ref[...]
    hidden = (0.5 * pre * (1.0 + lax.erf(pre * math.sqrt(0.5)))).astype(BF)
    half = o1_ref.shape[0]
    o1_ref[...] = hidden[:half]
    o2_ref[...] = hidden[half:]


def matmul_in(pieces, wa, wb, b):
    rows, depth = pieces[0].shape
    width = wa.shape[1]
    count = len(pieces)
    tokens = count * rows
    tile = 256
    return pl.pallas_call(
        mm1_kernel,
        grid=(width // tile,),
        in_specs=[pl.BlockSpec(memory_space=pl.ANY) for _ in pieces]
        + [
            pl.BlockSpec((wa.shape[0], tile), lambda i: (0, i)),
            pl.BlockSpec((wb.shape[0], tile), lambda i: (0, i)),
            pl.BlockSpec((1, tile), lambda i: (0, i)),
        ],
        out_specs=[pl.BlockSpec((tokens // 2, tile), lambda i: (0, i))] * 2,
        out_shape=[jax.ShapeDtypeStruct((tokens // 2, width), BF)] * 2,
        scratch_shapes=[pltpu.VMEM((tokens, depth), BF), pltpu.SemaphoreType.DMA((count,))],
        compiler_params=params(60),
        cost_estimate=pl.CostEstimate(
            flops=2 * tokens * depth * width,
            bytes_accessed=2 * (tokens * depth + depth * width),
            transcendentals=0,
        ),
    )(*pieces, wa, wb, b[None])


def mm2_kernel(*refs):
    hiddens, (own_ref, other_ref) = refs[:SIDE], refs[SIDE : SIDE + 2]
    outs, (left, sems) = refs[SIDE + 2 : -2], refs[-2:]
    fill(hiddens, left, sems)
    steps = pl.num_programs(0) // 2
    rows = outs[0].shape[0] // SIDE

    def part(w_ref):
        out = jnp.dot(left[...], w_ref[...], preferred_element_type=F32).astype(BF)
        for x in range(SIDE):
            for p, o_ref in enumerate(outs):
                at = (x * len(outs) + p) * rows
                o_ref[x * rows : (x + 1) * rows, :] = out[at : at + rows]

    pl.when(pl.program_id(0) < steps)(lambda: part(own_ref))
    pl.when(pl.program_id(0) >= steps)(lambda: part(other_ref))


def matmul_out(hiddens, own, other, count):
    depth, chans = own.shape
    tokens = SIDE * hiddens[0].shape[0]
    tile = 256
    steps = chans // tile
    return pl.pallas_call(
        mm2_kernel,
        grid=(2 * steps,),
        in_specs=[pl.BlockSpec(memory_space=pl.ANY)] * SIDE
        + [
            pl.BlockSpec((depth, tile), lambda i: (0, jnp.minimum(i, steps - 1))),
            pl.BlockSpec((depth, tile), lambda i: (0, jnp.maximum(i - steps, 0))),
        ],
        out_specs=[pl.BlockSpec((tokens // count, tile), lambda i: (0, i))] * count,
        out_shape=[jax.ShapeDtypeStruct((tokens // count, 2 * chans), BF)] * count,
        scratch_shapes=[pltpu.VMEM((tokens, depth), BF), pltpu.SemaphoreType.DMA((SIDE,))],
        compiler_params=params(32),
        cost_estimate=pl.CostEstimate(
            flops=4 * tokens * depth * chans,
            bytes_accessed=2 * (tokens * depth + 2 * depth * chans + 2 * tokens * chans),
            transcendentals=0,
        ),
    )(*hiddens, own, other)


def pair_kernel(a, b, o):
    o[...] = (a[...].astype(F32) + b[...].astype(F32)).astype(BF)


def add_pair(a, b):
    rows, width = a.shape
    block = pl.BlockSpec((rows // 2, width), lambda j: (j, 0))
    return pl.pallas_call(
        pair_kernel,
        grid=(2,),
        in_specs=[block] * 2,
        out_specs=block,
        out_shape=jax.ShapeDtypeStruct((rows, width), BF),
        compiler_params=params(16),
    )(a, b)


def add_kernel(half, a, b, c, *outs):
    total = a[...].astype(F32) + (b[...].astype(F32) + c[...].astype(F32))
    for s, o_ref in enumerate(outs):
        for x in range(total.shape[0] // (SIDE * half)):
            at = (x * SIDE + s) * half
            o_ref[x * half : (x + 1) * half, :] = total[at : at + half].astype(BF)


def add_pieces(half, *parts):
    rows, width = parts[0].shape
    return pl.pallas_call(
        functools.partial(add_kernel, half),
        grid=(2,),
        in_specs=[pl.BlockSpec((rows // 2, width), lambda j: (j, 0))] * len(parts),
        out_specs=[pl.BlockSpec((rows // SIDE // 2, width), lambda j: (j, 0))] * SIDE,
        out_shape=[jax.ShapeDtypeStruct((rows // SIDE, width), BF)] * SIDE,
        compiler_params=params(24),
    )(*parts)


def sum_kernel(a, b, c, d, own_ref, other_ref):
    chans = own_ref.shape[1]
    total = (a[...].astype(F32) + b[...].astype(F32)) + (c[...].astype(F32) + d[...].astype(F32))
    own_ref[...] = total[:, :chans]
    other_ref[...] = total[:, chans:].astype(BF)


def add_last(parts):
    rows, width = parts[0].shape
    return pl.pallas_call(
        sum_kernel,
        out_shape=[
            jax.ShapeDtypeStruct((rows, width // 2), F32),
            jax.ShapeDtypeStruct((rows, width // 2), BF),
        ],
        compiler_params=params(16),
    )(*parts)


def finish_kernel(place_ref, own1, own2, got1, got2, resid_ref, bias_ref, o_ref):
    half = o_ref.shape[1] // 2
    for i in range(2 * SIDE):
        at = pl.ds(i % SIDE * half, half)
        for k, part in enumerate((own1, own2) if i < SIDE else (got1, got2)):
            to = pl.ds(k * half, half)
            value = part[at, :].astype(F32) + resid_ref[place_ref[i], to, :] + bias_ref[...]
            o_ref[place_ref[i], to, :] = value.astype(BF)


def finish(place, own1, own2, got1, got2, resid, bias):
    return pl.pallas_call(
        finish_kernel,
        in_specs=[pl.BlockSpec(memory_space=pltpu.SMEM)] + [pl.BlockSpec(memory_space=pltpu.VMEM)] * 6,
        out_shape=jax.ShapeDtypeStruct(resid.shape, BF),
        compiler_params=params(16),
    )(place, own1, own2, got1, got2, resid, bias[None])


def exchange(a, axis):
    return lax.all_to_all(a, axis, split_axis=0, concat_axis=0, tiled=True)


def tie_kernel(*refs):
    pass


def tie(values, others):
    count = len(values)
    anywhere = pl.BlockSpec(memory_space=pl.ANY)
    return pl.pallas_call(
        tie_kernel,
        in_specs=[anywhere] * (count + len(others)),
        out_specs=[anywhere] * count,
        out_shape=[jax.ShapeDtypeStruct(v.shape, v.dtype) for v in values],
        input_output_aliases={i: i for i in range(count)},
        compiler_params=params(62),
    )(*values, *others)


def spectral(image, filter_bank, gain_first):
    rows_here, width, chans = image.shape
    groups = lax.axis_size("row")
    width_all = chans * lax.axis_size("col")
    tokens = rows_here * width
    one, two, three, four = spectral_tables(rows_here, width, rows_here * groups)
    high = lax.Precision.HIGH
    source = image.astype(F32).reshape(tokens, chans)
    sums, squares = lax.psum(
        (jnp.sum(source, axis=-1), jnp.sum(source * source, axis=-1)), "col"
    )
    mean = sums[:, None] / width_all
    square = squares[:, None] / width_all
    normed = (source - mean) / jnp.sqrt(square - mean * mean + 1e-05) * gain_first
    col = jnp.dot(one, normed, precision=high).astype(BF)
    col = exchange(col.reshape(groups, -1, chans), "row").reshape(-1, chans)
    spec = jnp.dot(two, col.astype(F32), precision=high)
    split = spec.shape[0] // 2
    spec_re, spec_im = spec[:split], spec[split:]
    f_re, f_im = filter_bank[0].reshape(-1, chans), filter_bank[1].reshape(-1, chans)
    filt = jnp.concatenate(
        [f_re * spec_re - f_im * spec_im, f_re * spec_im + f_im * spec_re], axis=0
    )
    back = jnp.dot(three, filt, precision=high).astype(BF)
    back = exchange(back.reshape(groups, -1, chans), "row").reshape(-1, chans)
    return source + jnp.dot(four, back.astype(F32), precision=high)


def three_parts(gain):
    top = lax.reduce_precision(gain, 8, 7)
    mid = lax.reduce_precision(gain - top, 8, 7)
    return jnp.stack([top, mid, gain - top - mid]).astype(BF)


def block_places():
    table = []
    for x in range(SIDE):
        for core in range(2):
            row = []
            for far in (False, True):
                at = core ^ far
                for step in (0, APART[at], OTHER[at], 2):
                    row.append((x + (step if step == 0 else -step)) % SIDE * 2 + at)
            table.append(row)
    return jnp.asarray(np.array(table, np.int32))[lax.axis_index("col")]


def gather_near(a, axis):
    far, *near = [hop(a, axis, (s, s)) for s in (2, 1, -1)]
    return jnp.stack([a, *near, far]).reshape(-1, a.shape[1])


def gather_far(a, axis):
    one, two = hop(a, axis, APART), hop(a, axis, OTHER)
    return [a, one, two, hop(one, axis, APART)]


def reduce_far(outs, large, small, half):
    own, fore, back, far = outs
    far = hop(far, large, OTHER)
    back = hop(back, large, APART)
    fore = hop(add_pair(fore, far), large, OTHER)
    return send_back(add_pieces(half, own, back, fore), small)


def send_back(parts, axis):
    far, *near = [hop(parts[i], axis, (s, s)) for i, s in ((3, 2), (1, -1), (2, 1))]
    return [parts[0], *near, far]


def on_device(image, filter_bank, gain_first, gain_second, w_in, b_in, w_out, b_out):
    rows_here, width, chans = image.shape
    cols = lax.axis_size("col")
    cut = w_in.shape[0] * 2 // 3
    w_in_low = lax.all_gather(w_in[:cut], "col", axis=0, tiled=True)
    resid = spectral(image, filter_bank, gain_first)
    tokens = rows_here * width
    own = tokens // cols
    half = own // 2
    extra = jnp.pad(three_parts(gain_second), ((0, half - 3), (0, 0)))
    message = jnp.concatenate(
        [
            resid.astype(BF).reshape(cols, own, chans),
            jnp.broadcast_to(extra[None], (cols, half, chans)),
        ],
        axis=1,
    )
    moved = exchange(message, "col")
    moved, w_rest, w_in_low = tie([moved, w_in[cut:], w_in_low], [])
    w_in_high = lax.all_gather(w_rest, "col", axis=0, tiled=True)
    first, second = normalize(moved, half, cut)
    first, second = gather_near(first, "z"), gather_near(second, "y")
    pieces = gather_far(first, "y") + gather_far(second, "z")
    hiddens = [gather_far(hidden, "x") for hidden in matmul_in(pieces, w_in_low, w_in_high, b_in)]
    other = swap_cores(w_out)
    sums = []
    for hidden, (large, small) in zip(hiddens, (("y", "z"), ("z", "y"))):
        outs = matmul_out(hidden, w_out, other, SIDE)
        sums.append(add_last(reduce_far(outs, large, small, half)))
    (own1, give1), (own2, give2) = sums
    got1, got2 = swap_cores(give1), swap_cores(give2)
    resid = resid.reshape(cols, own, chans)
    result = finish(block_places(), own1, own2, got1, got2, resid, b_out)
    return result.reshape(rows_here, width, chans)


def solution(mesh):
    placed = (
        P("row", None, "col"),
        P(None, None, "row", "col"),
        P("col"),
        P("col"),
        P("col", "row"),
        P("row"),
        P("row", "col"),
        P("col"),
    )
    return jax.shard_map(
        on_device, mesh=mesh, in_specs=placed, out_specs=P("row", None, "col"), check_vma=False
    )
```

```python
import functools
import math

import jax
import jax.numpy as jnp
import numpy as np
from jax import lax
from jax.experimental import pallas as pl
from jax.experimental.pallas import tpu as pltpu
from jax.sharding import PartitionSpec as P

SIDE = 4
BF = jnp.bfloat16
F32 = jnp.float32
MB = 1 << 20


def angles(count):
    index = np.arange(count)
    turn = (index[:, None] * index[None, :]) % count * (2.0 * math.pi / count)
    return np.cos(turn), np.sin(turn)


def spectral_tables(here, width, height):
    groups = height // here
    per = width // groups
    cos_w, sin_w = angles(width)
    cos_h, sin_h = angles(height)
    eye_r, eye_k = np.eye(here), np.eye(per)
    out = np.stack([cos_w, -sin_w]).reshape(2, width, groups, per)
    one = np.einsum("scqk,rt->qrsktc", out, eye_r).reshape(2 * here * width, here * width)
    turn = np.stack([np.stack([cos_h, sin_h]), np.stack([-sin_h, cos_h])])
    turn = turn.reshape(2, 2, groups, here, height)
    two = np.einsum("uvqrn,kl->unkqrvl", turn, eye_k).reshape(2 * height * per, 2 * height * per)
    back = np.stack([np.stack([cos_h, -sin_h]), np.stack([sin_h, cos_h])])
    back = back.reshape(2, 2, height, groups, here)
    three = np.einsum("uvnqr,kl->qrukvnl", back, eye_k).reshape(2 * height * per, 2 * height * per)
    four = np.einsum("sqkc,rt->rcqtsk", out.transpose(0, 2, 3, 1), eye_r)
    four = four.reshape(here * width, 2 * here * width) / (width * height)
    return [t.astype(np.float32) for t in (one, two, three, four)]


def hop(a, axis, steps):
    pairs = []
    for z in range(SIDE):
        for y in range(SIDE):
            for x in range(SIDE):
                for core, step in enumerate(steps):
                    to = {"z": z, "y": y, "x": x}
                    to[axis] = (to[axis] + step) % SIDE
                    source = ((z * SIDE + y) * SIDE + x) * 2 + core
                    pairs.append((source, ((to["z"] * SIDE + to["y"]) * SIDE + to["x"]) * 2 + core))
    return lax.ppermute(a, ("row", "col"), pairs)


APART = (1, -1)
OTHER = (-1, 1)


def swap_cores(a):
    pairs = [(x * 2 + core, x * 2 + 1 - core) for x in range(SIDE) for core in range(2)]
    return lax.ppermute(a, "col", pairs)


def params(mb):
    return pltpu.CompilerParams(vmem_limit_bytes=mb * MB)


def act_kernel(moved_ref, first_ref, second_ref):
    cols, _, chans = moved_ref.shape
    half = first_ref.shape[0]
    values = moved_ref[:, : 2 * half, :].astype(F32)
    gains = jnp.sum(moved_ref[:, 2 * half :, :].astype(F32)[:, :3], axis=1)
    mean = jnp.sum(jnp.sum(values, axis=0), axis=-1, keepdims=True) / (cols * chans)
    square = jnp.sum(jnp.sum(values * values, axis=0), axis=-1, keepdims=True) / (cols * chans)
    scale = 1.0 / jnp.sqrt(square - mean * mean + 1e-05)
    for j in range(cols):
        part = ((values[j] - mean) * scale * gains[j][None, :]).astype(BF)
        first_ref[:, j * chans : (j + 1) * chans] = part[:half]
        second_ref[:, j * chans : (j + 1) * chans] = part[half:]


def normalize(moved, half):
    cols, _, chans = moved.shape
    shape = jax.ShapeDtypeStruct((half, cols * chans), BF)
    return pl.pallas_call(act_kernel, out_shape=(shape, shape), compiler_params=params(16))(moved)


def fill(sources, target, sems):
    rows = target.shape[0] // len(sources)
    copies = [
        pltpu.make_async_copy(source, target.at[pl.ds(i * rows, rows)], sems.at[i])
        for i, source in enumerate(sources)
    ]

    @pl.when(pl.program_id(0) == 0)
    def _():
        for copy in copies:
            copy.start()
        for copy in copies:
            copy.wait()


def mm1_kernel(count, *refs):
    pieces, (w_ref, b_ref), (o1_ref, o2_ref, left, sems) = refs[:count], refs[count : count + 2], refs[-4:]
    fill(pieces, left, sems)
    pre = jnp.dot(left[...], w_ref[...], preferred_element_type=F32) + b_ref[...]
    hidden = (0.5 * pre * (1.0 + lax.erf(pre * math.sqrt(0.5)))).astype(BF)
    half = o1_ref.shape[0]
    o1_ref[...] = hidden[:half]
    o2_ref[...] = hidden[half:]


def matmul_in(first, second, w, b, total, into=()):
    pieces = [*first, *second]
    rows, depth = pieces[0].shape
    width = w.shape[1]
    count = len(pieces)
    tile = 256
    block = len(first) * rows
    at = total // block - 1 if into else 0
    anywhere = pl.BlockSpec(memory_space=pl.ANY)
    return pl.pallas_call(
        functools.partial(mm1_kernel, count),
        grid=(width // tile,),
        in_specs=[anywhere] * count
        + [pl.BlockSpec((depth, tile), lambda i: (0, i)), pl.BlockSpec((1, tile), lambda i: (0, i))]
        + [anywhere] * len(into),
        out_specs=[pl.BlockSpec((block, tile), lambda i: (at, i))] * 2,
        out_shape=[jax.ShapeDtypeStruct((total, width), BF)] * 2,
        input_output_aliases={count + 2 + i: i for i in range(len(into))},
        scratch_shapes=[pltpu.VMEM((count * rows, depth), BF), pltpu.SemaphoreType.DMA((count,))],
        compiler_params=params(58),
        cost_estimate=pl.CostEstimate(
            flops=2 * count * rows * depth * width,
            bytes_accessed=2 * (count * rows * depth + depth * width),
            transcendentals=0,
        ),
    )(*pieces, w, b[None], *into)


def mm2_kernel(count, *refs):
    hiddens, (own_ref, other_ref) = refs[:count], refs[count : count + 2]
    outs, (left, sems) = refs[-2 - SIDE : -2], refs[-2:]
    fill(hiddens, left, sems)
    steps = pl.num_programs(0) // 2
    rows = outs[0].shape[0] // count

    def part(w_ref):
        out = jnp.dot(left[...], w_ref[...], preferred_element_type=F32).astype(BF)
        for x in range(count):
            for p, o_ref in enumerate(outs):
                at = (x * len(outs) + p) * rows
                o_ref[x * rows : (x + 1) * rows, :] = out[at : at + rows]

    pl.when(pl.program_id(0) < steps)(lambda: part(own_ref))
    pl.when(pl.program_id(0) >= steps)(lambda: part(other_ref))


def matmul_out(hiddens, own, other, into=()):
    depth, chans = own.shape
    count = len(hiddens)
    tokens = count * hiddens[0].shape[0]
    total = hiddens[0].shape[0]
    tile = 256
    steps = chans // tile
    block = tokens // SIDE
    at = SIDE - 1 if into else 0
    anywhere = pl.BlockSpec(memory_space=pl.ANY)
    return pl.pallas_call(
        functools.partial(mm2_kernel, count),
        grid=(2 * steps,),
        in_specs=[anywhere] * count
        + [
            pl.BlockSpec((depth, tile), lambda i: (0, jnp.minimum(i, steps - 1))),
            pl.BlockSpec((depth, tile), lambda i: (0, jnp.maximum(i - steps, 0))),
        ]
        + [anywhere] * len(into),
        out_specs=[pl.BlockSpec((block, tile), lambda i: (at, i))] * SIDE,
        out_shape=[jax.ShapeDtypeStruct((total, 2 * chans), BF)] * SIDE,
        input_output_aliases={count + 2 + i: i for i in range(len(into))},
        scratch_shapes=[pltpu.VMEM((tokens, depth), BF), pltpu.SemaphoreType.DMA((count,))],
        compiler_params=params(58),
        cost_estimate=pl.CostEstimate(
            flops=4 * tokens * depth * chans,
            bytes_accessed=2 * (tokens * depth + 2 * depth * chans + 2 * tokens * chans),
            transcendentals=0,
        ),
    )(*hiddens, own, other, *into)


def pair_kernel(a, b, o):
    o[...] = (a[...].astype(F32) + b[...].astype(F32)).astype(BF)


def add_pair(a, b):
    rows, width = a.shape
    block = pl.BlockSpec((rows // 2, width), lambda j: (j, 0))
    return pl.pallas_call(
        pair_kernel,
        grid=(2,),
        in_specs=[block] * 2,
        out_specs=block,
        out_shape=jax.ShapeDtypeStruct((rows, width), BF),
        compiler_params=params(16),
    )(a, b)


def add_kernel(half, a, b, c, *outs):
    total = a[...].astype(F32) + (b[...].astype(F32) + c[...].astype(F32))
    for s, o_ref in enumerate(outs):
        for x in range(total.shape[0] // (SIDE * half)):
            at = (x * SIDE + s) * half
            o_ref[x * half : (x + 1) * half, :] = total[at : at + half].astype(BF)


def add_pieces(half, *parts):
    rows, width = parts[0].shape
    return pl.pallas_call(
        functools.partial(add_kernel, half),
        grid=(2,),
        in_specs=[pl.BlockSpec((rows // 2, width), lambda j: (j, 0))] * len(parts),
        out_specs=[pl.BlockSpec((rows // SIDE // 2, width), lambda j: (j, 0))] * SIDE,
        out_shape=[jax.ShapeDtypeStruct((rows // SIDE, width), BF)] * SIDE,
        compiler_params=params(24),
    )(*parts)


def sum_kernel(a, b, c, d, own_ref, other_ref):
    chans = own_ref.shape[1]
    total = (a[...].astype(F32) + b[...].astype(F32)) + (c[...].astype(F32) + d[...].astype(F32))
    own_ref[...] = total[:, :chans]
    other_ref[...] = total[:, chans:].astype(BF)


def add_last(parts):
    rows, width = parts[0].shape
    return pl.pallas_call(
        sum_kernel,
        out_shape=[
            jax.ShapeDtypeStruct((rows, width // 2), F32),
            jax.ShapeDtypeStruct((rows, width // 2), BF),
        ],
        compiler_params=params(16),
    )(*parts)


def finish_kernel(place_ref, own1, own2, got1, got2, resid_ref, bias_ref, o_ref):
    half = o_ref.shape[1] // 2
    for i in range(2 * SIDE):
        at = pl.ds(i % SIDE * half, half)
        for k, part in enumerate((own1, own2) if i < SIDE else (got1, got2)):
            to = pl.ds(k * half, half)
            value = part[at, :].astype(F32) + resid_ref[place_ref[i], to, :] + bias_ref[...]
            o_ref[place_ref[i], to, :] = value.astype(BF)


def finish(place, own1, own2, got1, got2, resid, bias):
    return pl.pallas_call(
        finish_kernel,
        in_specs=[pl.BlockSpec(memory_space=pltpu.SMEM)] + [pl.BlockSpec(memory_space=pltpu.VMEM)] * 6,
        out_shape=jax.ShapeDtypeStruct(resid.shape, BF),
        compiler_params=params(16),
    )(place, own1, own2, got1, got2, resid, bias[None])


def exchange(a, axis):
    return lax.all_to_all(a, axis, split_axis=0, concat_axis=0, tiled=True)


def tie_kernel(*refs):
    pass


def tie(values, others):
    count = len(values)
    anywhere = pl.BlockSpec(memory_space=pl.ANY)
    return pl.pallas_call(
        tie_kernel,
        in_specs=[anywhere] * (count + len(others)),
        out_specs=[anywhere] * count,
        out_shape=[jax.ShapeDtypeStruct(v.shape, v.dtype) for v in values],
        input_output_aliases={i: i for i in range(count)},
        compiler_params=params(62),
    )(*values, *others)


def spectral(image, filter_bank, gain_first):
    rows_here, width, chans = image.shape
    groups = lax.axis_size("row")
    width_all = chans * lax.axis_size("col")
    tokens = rows_here * width
    one, two, three, four = spectral_tables(rows_here, width, rows_here * groups)
    high = lax.Precision.HIGH
    source = image.astype(F32).reshape(tokens, chans)
    sums, squares = lax.psum(
        (jnp.sum(source, axis=-1), jnp.sum(source * source, axis=-1)), "col"
    )
    mean = sums[:, None] / width_all
    square = squares[:, None] / width_all
    normed = (source - mean) / jnp.sqrt(square - mean * mean + 1e-05) * gain_first
    col = jnp.dot(one, normed, precision=high).astype(BF)
    col = exchange(col.reshape(groups, -1, chans), "row").reshape(-1, chans)
    spec = jnp.dot(two, col.astype(F32), precision=high)
    split = spec.shape[0] // 2
    spec_re, spec_im = spec[:split], spec[split:]
    f_re, f_im = filter_bank[0].reshape(-1, chans), filter_bank[1].reshape(-1, chans)
    filt = jnp.concatenate(
        [f_re * spec_re - f_im * spec_im, f_re * spec_im + f_im * spec_re], axis=0
    )
    back = jnp.dot(three, filt, precision=high).astype(BF)
    back = exchange(back.reshape(groups, -1, chans), "row").reshape(-1, chans)
    return source + jnp.dot(four, back.astype(F32), precision=high)


def three_parts(gain):
    top = lax.reduce_precision(gain, 8, 7)
    mid = lax.reduce_precision(gain - top, 8, 7)
    return jnp.stack([top, mid, gain - top - mid]).astype(BF)


def block_places():
    table = []
    for x in range(SIDE):
        for core in range(2):
            row = []
            for far in (False, True):
                at = core ^ far
                for step in (0, APART[at], OTHER[at], 2):
                    row.append((x + (step if step == 0 else -step)) % SIDE * 2 + at)
            table.append(row)
    return jnp.asarray(np.array(table, np.int32))[lax.axis_index("col")]


def gather_near(a, axis):
    far, *near = [hop(a, axis, (s, s)) for s in (2, 1, -1)]
    return jnp.stack([a, *near, far]).reshape(-1, a.shape[1])


def gather_far(a, axis):
    one, two = hop(a, axis, APART), hop(a, axis, OTHER)
    return [a, one, two, hop(one, axis, APART)]


def reduce_far(outs, large, small, half):
    own, fore, back, far = outs
    far = hop(far, large, OTHER)
    back = hop(back, large, APART)
    fore = hop(add_pair(fore, far), large, OTHER)
    return send_back(add_pieces(half, own, back, fore), small)


def send_back(parts, axis):
    far, *near = [hop(parts[i], axis, (s, s)) for i, s in ((3, 2), (1, -1), (2, 1))]
    return [parts[0], *near, far]


def on_device(image, filter_bank, gain_first, gain_second, w_in, b_in, w_out, b_out):
    rows_here, width, chans = image.shape
    cols = lax.axis_size("col")
    w_in_all = lax.all_gather(w_in, "col", axis=0, tiled=True)
    resid = spectral(image, filter_bank, gain_first)
    tokens = rows_here * width
    own = tokens // cols
    half = own // 2
    extra = jnp.pad(three_parts(gain_second), ((0, half - 3), (0, 0)))
    message = jnp.concatenate(
        [
            resid.astype(BF).reshape(cols, own, chans),
            jnp.broadcast_to(extra[None], (cols, half, chans)),
        ],
        axis=1,
    )
    moved = exchange(message, "col")
    first, second = normalize(moved, half)
    first, second = gather_near(first, "z"), gather_near(second, "y")
    first, second = gather_far(first, "y"), gather_far(second, "z")
    total = SIDE * SIDE * half
    hidden = matmul_in(first[:-1], second[:-1], w_in_all, b_in, total)
    hidden = matmul_in(first[-1:], second[-1:], w_in_all, b_in, total, hidden)
    other = swap_cores(w_out)
    hiddens = [gather_far(h, "x") for h in hidden]
    outs = [matmul_out(h[:-1], w_out, other) for h in hiddens]
    outs = [matmul_out(h[-1:], w_out, other, out) for h, out in zip(hiddens, outs)]
    sums = []
    for out, (large, small) in zip(outs, (("y", "z"), ("z", "y"))):
        sums.append(add_last(reduce_far(out, large, small, half)))
    (own1, give1), (own2, give2) = sums
    got1, got2 = swap_cores(give1), swap_cores(give2)
    resid = resid.reshape(cols, own, chans)
    result = finish(block_places(), own1, own2, got1, got2, resid, b_out)
    return result.reshape(rows_here, width, chans)


def solution(mesh):
    placed = (
        P("row", None, "col"),
        P(None, None, "row", "col"),
        P("col"),
        P("col"),
        P("col", "row"),
        P("row"),
        P("row", "col"),
        P("col"),
    )
    return jax.shard_map(
        on_device, mesh=mesh, in_specs=placed, out_specs=P("row", None, "col"), check_vma=False
    )
```

```python
import functools
import math

import jax
import jax.numpy as jnp
import numpy as np
from jax import lax
from jax.experimental import pallas as pl
from jax.experimental.pallas import tpu as pltpu
from jax.sharding import PartitionSpec as P

SIDE = 4
BF = jnp.bfloat16
F32 = jnp.float32
MB = 1 << 20


def angles(count):
    index = np.arange(count)
    turn = (index[:, None] * index[None, :]) % count * (2.0 * math.pi / count)
    return np.cos(turn), np.sin(turn)


def spectral_tables(here, width, height):
    groups = height // here
    per = width // groups
    cos_w, sin_w = angles(width)
    cos_h, sin_h = angles(height)
    eye_r, eye_k = np.eye(here), np.eye(per)
    out = np.stack([cos_w, -sin_w]).reshape(2, width, groups, per)
    one = np.einsum("scqk,rt->qrsktc", out, eye_r).reshape(2 * here * width, here * width)
    turn = np.stack([np.stack([cos_h, sin_h]), np.stack([-sin_h, cos_h])])
    turn = turn.reshape(2, 2, groups, here, height)
    two = np.einsum("uvqrn,kl->unkqrvl", turn, eye_k).reshape(2 * height * per, 2 * height * per)
    back = np.stack([np.stack([cos_h, -sin_h]), np.stack([sin_h, cos_h])])
    back = back.reshape(2, 2, height, groups, here)
    three = np.einsum("uvnqr,kl->qrukvnl", back, eye_k).reshape(2 * height * per, 2 * height * per)
    four = np.einsum("sqkc,rt->rcqtsk", out.transpose(0, 2, 3, 1), eye_r)
    four = four.reshape(here * width, 2 * here * width) / (width * height)
    return [t.astype(np.float32) for t in (one, two, three, four)]


def hop(a, axis, steps):
    pairs = []
    for z in range(SIDE):
        for y in range(SIDE):
            for x in range(SIDE):
                for core, step in enumerate(steps):
                    to = {"z": z, "y": y, "x": x}
                    to[axis] = (to[axis] + step) % SIDE
                    source = ((z * SIDE + y) * SIDE + x) * 2 + core
                    pairs.append((source, ((to["z"] * SIDE + to["y"]) * SIDE + to["x"]) * 2 + core))
    return lax.ppermute(a, ("row", "col"), pairs)


APART = (1, -1)
OTHER = (-1, 1)


def swap_cores(a):
    pairs = [(x * 2 + core, x * 2 + 1 - core) for x in range(SIDE) for core in range(2)]
    return lax.ppermute(a, "col", pairs)


def params(mb):
    return pltpu.CompilerParams(vmem_limit_bytes=mb * MB)


def act_kernel(moved_ref, gain_ref, first_ref, second_ref):
    cols, _, chans = moved_ref.shape
    half = first_ref.shape[0]
    values = moved_ref[...].astype(F32)
    mean = jnp.sum(jnp.sum(values, axis=0), axis=-1, keepdims=True) / (cols * chans)
    square = jnp.sum(jnp.sum(values * values, axis=0), axis=-1, keepdims=True) / (cols * chans)
    scale = 1.0 / jnp.sqrt(square - mean * mean + 1e-05)
    for j in range(cols):
        part = ((values[j] - mean) * scale * gain_ref[j : j + 1, :]).astype(BF)
        first_ref[:, j * chans : (j + 1) * chans] = part[:half]
        second_ref[:, j * chans : (j + 1) * chans] = part[half:]


def normalize(moved, gains, half):
    cols, _, chans = moved.shape
    shape = jax.ShapeDtypeStruct((half, cols * chans), BF)
    return pl.pallas_call(act_kernel, out_shape=(shape, shape), compiler_params=params(16))(moved, gains)


def mm1_kernel(*refs):
    pieces, (w_ref, b_ref, o_ref) = refs[:-3], refs[-3:]
    left = jnp.concatenate([p[...] for p in pieces], axis=0)
    pre = jnp.dot(left, w_ref[...], preferred_element_type=F32) + b_ref[...]
    o_ref[...] = (0.5 * pre * (1.0 + lax.erf(pre * math.sqrt(0.5)))).astype(BF)


def matmul_in(pieces, w, b):
    depth, width = w.shape
    rows = pieces[0].shape[0]
    tokens = len(pieces) * rows
    tile = 256
    return pl.pallas_call(
        mm1_kernel,
        grid=(width // tile,),
        in_specs=[pl.BlockSpec((rows, depth), lambda i: (0, 0)) for _ in pieces]
        + [
            pl.BlockSpec((depth, tile), lambda i: (0, i)),
            pl.BlockSpec((1, tile), lambda i: (0, i)),
        ],
        out_specs=pl.BlockSpec((tokens, tile), lambda i: (0, i)),
        out_shape=jax.ShapeDtypeStruct((tokens, width), BF),
        compiler_params=params(58),
        cost_estimate=pl.CostEstimate(
            flops=2 * tokens * depth * width,
            bytes_accessed=2 * (tokens * depth + depth * width),
            transcendentals=0,
        ),
    )(*pieces, w, b[None])


def fill(sources, target, sems):
    rows = target.shape[0] // len(sources)
    copies = [
        pltpu.make_async_copy(source, target.at[pl.ds(i * rows, rows)], sems.at[i])
        for i, source in enumerate(sources)
    ]

    @pl.when(pl.program_id(0) == 0)
    def _():
        for copy in copies:
            copy.start()
        for copy in copies:
            copy.wait()


def mm2_kernel(*refs):
    hiddens, (own_ref, other_ref) = refs[:SIDE], refs[SIDE : SIDE + 2]
    outs, (left, sems) = refs[SIDE + 2 : -2], refs[-2:]
    fill(hiddens, left, sems)
    steps = pl.num_programs(0) // 2
    rows = outs[0].shape[0] // SIDE

    def part(w_ref):
        out = jnp.dot(left[...], w_ref[...], preferred_element_type=F32).astype(BF)
        for x in range(SIDE):
            for p, o_ref in enumerate(outs):
                at = (x * len(outs) + p) * rows
                o_ref[x * rows : (x + 1) * rows, :] = out[at : at + rows]

    pl.when(pl.program_id(0) < steps)(lambda: part(own_ref))
    pl.when(pl.program_id(0) >= steps)(lambda: part(other_ref))


def matmul_out(hiddens, own, other, count):
    depth, chans = own.shape
    tokens = SIDE * hiddens[0].shape[0]
    tile = 256
    steps = chans // tile
    return pl.pallas_call(
        mm2_kernel,
        grid=(2 * steps,),
        in_specs=[pl.BlockSpec(memory_space=pl.ANY)] * SIDE
        + [
            pl.BlockSpec((depth, tile), lambda i: (0, jnp.minimum(i, steps - 1))),
            pl.BlockSpec((depth, tile), lambda i: (0, jnp.maximum(i - steps, 0))),
        ],
        out_specs=[pl.BlockSpec((tokens // count, tile), lambda i: (0, i))] * count,
        out_shape=[jax.ShapeDtypeStruct((tokens // count, 2 * chans), BF)] * count,
        scratch_shapes=[pltpu.VMEM((tokens, depth), BF), pltpu.SemaphoreType.DMA((SIDE,))],
        compiler_params=params(32),
        cost_estimate=pl.CostEstimate(
            flops=4 * tokens * depth * chans,
            bytes_accessed=2 * (tokens * depth + 2 * depth * chans + 2 * tokens * chans),
            transcendentals=0,
        ),
    )(*hiddens, own, other)


def pair_kernel(a, b, o):
    o[...] = (a[...].astype(F32) + b[...].astype(F32)).astype(BF)


def add_pair(a, b):
    rows, width = a.shape
    block = pl.BlockSpec((rows // 2, width), lambda j: (j, 0))
    return pl.pallas_call(
        pair_kernel,
        grid=(2,),
        in_specs=[block] * 2,
        out_specs=block,
        out_shape=jax.ShapeDtypeStruct((rows, width), BF),
        compiler_params=params(16),
    )(a, b)


def add_kernel(half, a, b, c, *outs):
    total = a[...].astype(F32) + (b[...].astype(F32) + c[...].astype(F32))
    for s, o_ref in enumerate(outs):
        for x in range(total.shape[0] // (SIDE * half)):
            at = (x * SIDE + s) * half
            o_ref[x * half : (x + 1) * half, :] = total[at : at + half].astype(BF)


def add_pieces(half, *parts):
    rows, width = parts[0].shape
    return pl.pallas_call(
        functools.partial(add_kernel, half),
        grid=(2,),
        in_specs=[pl.BlockSpec((rows // 2, width), lambda j: (j, 0))] * len(parts),
        out_specs=[pl.BlockSpec((rows // SIDE // 2, width), lambda j: (j, 0))] * SIDE,
        out_shape=[jax.ShapeDtypeStruct((rows // SIDE, width), BF)] * SIDE,
        compiler_params=params(24),
    )(*parts)


def sum_kernel(a, b, c, d, own_ref, other_ref):
    chans = own_ref.shape[1]
    total = (a[...].astype(F32) + b[...].astype(F32)) + (c[...].astype(F32) + d[...].astype(F32))
    own_ref[...] = total[:, :chans]
    other_ref[...] = total[:, chans:].astype(BF)


def add_last(parts):
    rows, width = parts[0].shape
    return pl.pallas_call(
        sum_kernel,
        out_shape=[
            jax.ShapeDtypeStruct((rows, width // 2), F32),
            jax.ShapeDtypeStruct((rows, width // 2), BF),
        ],
        compiler_params=params(16),
    )(*parts)


def finish_kernel(place_ref, own1, own2, got1, got2, resid_ref, bias_ref, o_ref):
    half = o_ref.shape[1] // 2
    for i in range(2 * SIDE):
        at = pl.ds(i % SIDE * half, half)
        for k, part in enumerate((own1, own2) if i < SIDE else (got1, got2)):
            to = pl.ds(k * half, half)
            value = part[at, :].astype(F32) + resid_ref[place_ref[i], to, :] + bias_ref[...]
            o_ref[place_ref[i], to, :] = value.astype(BF)


def finish(place, own1, own2, got1, got2, resid, bias):
    return pl.pallas_call(
        finish_kernel,
        in_specs=[pl.BlockSpec(memory_space=pltpu.SMEM)] + [pl.BlockSpec(memory_space=pltpu.VMEM)] * 6,
        out_shape=jax.ShapeDtypeStruct(resid.shape, BF),
        compiler_params=params(16),
    )(place, own1, own2, got1, got2, resid, bias[None])


def exchange(a, axis):
    return lax.all_to_all(a, axis, split_axis=0, concat_axis=0, tiled=True)


def tie_kernel(*refs):
    pass


def tie(values, others):
    count = len(values)
    anywhere = pl.BlockSpec(memory_space=pl.ANY)
    return pl.pallas_call(
        tie_kernel,
        in_specs=[anywhere] * (count + len(others)),
        out_specs=[anywhere] * count,
        out_shape=[jax.ShapeDtypeStruct(v.shape, v.dtype) for v in values],
        input_output_aliases={i: i for i in range(count)},
        compiler_params=params(62),
    )(*values, *others)


def spectral(image, filter_bank, gain_first, early):
    rows_here, width, chans = image.shape
    groups = lax.axis_size("row")
    width_all = chans * lax.axis_size("col")
    tokens = rows_here * width
    one, two, three, four = spectral_tables(rows_here, width, rows_here * groups)
    high = lax.Precision.HIGH
    source = image.astype(F32).reshape(tokens, chans)
    sums, squares = lax.psum(
        (jnp.sum(source, axis=-1), jnp.sum(source * source, axis=-1)), "col"
    )
    mean = sums[:, None] / width_all
    square = squares[:, None] / width_all
    normed = (source - mean) / jnp.sqrt(square - mean * mean + 1e-05) * gain_first
    col = jnp.dot(one, normed, precision=high).astype(BF)
    col = exchange(col.reshape(groups, -1, chans), "row").reshape(-1, chans)
    (col,) = tie([col], early)
    spec = jnp.dot(two, col.astype(F32), precision=high)
    split = spec.shape[0] // 2
    spec_re, spec_im = spec[:split], spec[split:]
    f_re, f_im = filter_bank[0].reshape(-1, chans), filter_bank[1].reshape(-1, chans)
    filt = jnp.concatenate(
        [f_re * spec_re - f_im * spec_im, f_re * spec_im + f_im * spec_re], axis=0
    )
    back = jnp.dot(three, filt, precision=high).astype(BF)
    back = exchange(back.reshape(groups, -1, chans), "row").reshape(-1, chans)
    return source + jnp.dot(four, back.astype(F32), precision=high)


def block_places():
    table = []
    for x in range(SIDE):
        for core in range(2):
            row = []
            for far in (False, True):
                at = core ^ far
                for step in (0, APART[at], OTHER[at], 2):
                    row.append((x + (step if step == 0 else -step)) % SIDE * 2 + at)
            table.append(row)
    return jnp.asarray(np.array(table, np.int32))[lax.axis_index("col")]


def gather_near(a, axis):
    far, *near = [hop(a, axis, (s, s)) for s in (2, 1, -1)]
    return jnp.stack([a, *near, far]).reshape(-1, a.shape[1])


def gather_far(a, axis):
    one, two = hop(a, axis, APART), hop(a, axis, OTHER)
    return [a, one, two, hop(one, axis, APART)]


def gather_gains(gain):
    pair = jnp.stack([gain, swap_cores(gain)])
    rows = jnp.concatenate(gather_far(pair, "x"))
    table = []
    for x in range(SIDE):
        for core in range(2):
            steps = (0, APART[core], OTHER[core], 2)
            table.append([(x - s) % SIDE * 2 + (core ^ k) for s in steps for k in range(2)])
    places = jnp.asarray(np.array(table, np.int32))[lax.axis_index("col")]
    count = rows.shape[0]
    mine = lax.broadcasted_iota(jnp.int32, (count, count), 0) == places[None, :]
    return jnp.sum(jnp.where(mine[:, :, None], rows[None], 0.0), axis=1)


def reduce_far(outs, large, small, half):
    own, fore, back, far = outs
    far = hop(far, large, OTHER)
    back = hop(back, large, APART)
    fore = hop(add_pair(fore, far), large, OTHER)
    return send_back(add_pieces(half, own, back, fore), small)


def send_back(parts, axis):
    far, *near = [hop(parts[i], axis, (s, s)) for i, s in ((3, 2), (1, -1), (2, 1))]
    return [parts[0], *near, far]


def on_device(image, filter_bank, gain_first, gain_second, w_in, b_in, w_out, b_out):
    rows_here, width, chans = image.shape
    cols = lax.axis_size("col")
    w_in_all = lax.all_gather(w_in, "col", axis=0, tiled=True)
    gains = gather_gains(gain_second)
    resid = spectral(image, filter_bank, gain_first, [gains])
    tokens = rows_here * width
    own = tokens // cols
    half = own // 2
    moved = exchange(resid.astype(BF).reshape(cols, own, chans), "col")
    first, second = normalize(moved, gains, half)
    first, second = gather_near(first, "z"), gather_near(second, "y")
    parts = [gather_far(first, "y"), gather_far(second, "z")]
    hiddens = [gather_far(matmul_in(part, w_in_all, b_in), "x") for part in parts]
    other = swap_cores(w_out)
    sums = []
    for hidden, (large, small) in zip(hiddens, (("y", "z"), ("z", "y"))):
        outs = matmul_out(hidden, w_out, other, SIDE)
        sums.append(add_last(reduce_far(outs, large, small, half)))
    (own1, give1), (own2, give2) = sums
    got1, got2 = swap_cores(give1), swap_cores(give2)
    resid = resid.reshape(cols, own, chans)
    result = finish(block_places(), own1, own2, got1, got2, resid, b_out)
    return result.reshape(rows_here, width, chans)


def solution(mesh):
    placed = (
        P("row", None, "col"),
        P(None, None, "row", "col"),
        P("col"),
        P("col"),
        P("col", "row"),
        P("row"),
        P("row", "col"),
        P("col"),
    )
    return jax.shard_map(
        on_device, mesh=mesh, in_specs=placed, out_specs=P("row", None, "col"), check_vma=False
    )
```

```python
import functools
import math

import jax
import jax.numpy as jnp
import numpy as np
from jax import lax
from jax.experimental import pallas as pl
from jax.experimental.pallas import tpu as pltpu
from jax.sharding import PartitionSpec as P

SIDE = 4
BF = jnp.bfloat16
F32 = jnp.float32
MB = 1 << 20


def angles(count):
    index = np.arange(count)
    turn = (index[:, None] * index[None, :]) % count * (2.0 * math.pi / count)
    return np.cos(turn), np.sin(turn)


def spectral_tables(here, width, height):
    groups = height // here
    per = width // groups
    cos_w, sin_w = angles(width)
    cos_h, sin_h = angles(height)
    eye_r, eye_k = np.eye(here), np.eye(per)
    out = np.stack([cos_w, -sin_w]).reshape(2, width, groups, per)
    one = np.einsum("scqk,rt->qrsktc", out, eye_r).reshape(2 * here * width, here * width)
    turn = np.stack([np.stack([cos_h, sin_h]), np.stack([-sin_h, cos_h])])
    turn = turn.reshape(2, 2, groups, here, height)
    two = np.einsum("uvqrn,kl->unkqrvl", turn, eye_k).reshape(2 * height * per, 2 * height * per)
    back = np.stack([np.stack([cos_h, -sin_h]), np.stack([sin_h, cos_h])])
    back = back.reshape(2, 2, height, groups, here)
    three = np.einsum("uvnqr,kl->qrukvnl", back, eye_k).reshape(2 * height * per, 2 * height * per)
    four = np.einsum("sqkc,rt->rcqtsk", out.transpose(0, 2, 3, 1), eye_r)
    four = four.reshape(here * width, 2 * here * width) / (width * height)
    return [t.astype(np.float32) for t in (one, two, three, four)]


def hop(a, axis, steps):
    pairs = []
    for z in range(SIDE):
        for y in range(SIDE):
            for x in range(SIDE):
                for core, step in enumerate(steps):
                    to = {"z": z, "y": y, "x": x}
                    to[axis] = (to[axis] + step) % SIDE
                    source = ((z * SIDE + y) * SIDE + x) * 2 + core
                    pairs.append((source, ((to["z"] * SIDE + to["y"]) * SIDE + to["x"]) * 2 + core))
    return lax.ppermute(a, ("row", "col"), pairs)


APART = (1, -1)
OTHER = (-1, 1)


def swap_cores(a):
    pairs = [(x * 2 + core, x * 2 + 1 - core) for x in range(SIDE) for core in range(2)]
    return lax.ppermute(a, "col", pairs)


def params(mb):
    return pltpu.CompilerParams(vmem_limit_bytes=mb * MB)


def act_kernel(moved_ref, gain_ref, first_ref, second_ref):
    cols, _, chans = moved_ref.shape
    half = first_ref.shape[0]
    values = moved_ref[...].astype(F32)
    mean = jnp.sum(jnp.sum(values, axis=0), axis=-1, keepdims=True) / (cols * chans)
    square = jnp.sum(jnp.sum(values * values, axis=0), axis=-1, keepdims=True) / (cols * chans)
    scale = 1.0 / jnp.sqrt(square - mean * mean + 1e-05)
    for j in range(cols):
        part = ((values[j] - mean) * scale * gain_ref[j : j + 1, :]).astype(BF)
        first_ref[:, j * chans : (j + 1) * chans] = part[:half]
        second_ref[:, j * chans : (j + 1) * chans] = part[half:]


def normalize(moved, gains, half):
    cols, _, chans = moved.shape
    shape = jax.ShapeDtypeStruct((half, cols * chans), BF)
    return pl.pallas_call(act_kernel, out_shape=(shape, shape), compiler_params=params(16))(moved, gains)


def mm1_kernel(*refs):
    pieces, (w_ref, b_ref, o_ref) = refs[:-3], refs[-3:]
    left = jnp.concatenate([p[...] for p in pieces], axis=0)
    pre = jnp.dot(left, w_ref[...], preferred_element_type=F32) + b_ref[...]
    o_ref[...] = (0.5 * pre * (1.0 + lax.erf(pre * math.sqrt(0.5)))).astype(BF)


def matmul_in(pieces, w, b):
    depth, width = w.shape
    rows = pieces[0].shape[0]
    tokens = len(pieces) * rows
    tile = 256
    return pl.pallas_call(
        mm1_kernel,
        grid=(width // tile,),
        in_specs=[pl.BlockSpec((rows, depth), lambda i: (0, 0)) for _ in pieces]
        + [
            pl.BlockSpec((depth, tile), lambda i: (0, i)),
            pl.BlockSpec((1, tile), lambda i: (0, i)),
        ],
        out_specs=pl.BlockSpec((tokens, tile), lambda i: (0, i)),
        out_shape=jax.ShapeDtypeStruct((tokens, width), BF),
        compiler_params=params(58),
        cost_estimate=pl.CostEstimate(
            flops=2 * tokens * depth * width,
            bytes_accessed=2 * (tokens * depth + depth * width),
            transcendentals=0,
        ),
    )(*pieces, w, b[None])


def fill(sources, target, sems):
    rows = target.shape[0] // len(sources)
    copies = [
        pltpu.make_async_copy(source, target.at[pl.ds(i * rows, rows)], sems.at[i])
        for i, source in enumerate(sources)
    ]

    @pl.when(pl.program_id(0) == 0)
    def _():
        for copy in copies:
            copy.start()
        for copy in copies:
            copy.wait()


def mm2_kernel(*refs):
    hiddens, (own_ref, other_ref) = refs[:SIDE], refs[SIDE : SIDE + 2]
    outs, (left, sems) = refs[SIDE + 2 : -2], refs[-2:]
    fill(hiddens, left, sems)
    steps = pl.num_programs(0) // 2
    rows = outs[0].shape[0] // SIDE

    def part(w_ref):
        out = jnp.dot(left[...], w_ref[...], preferred_element_type=F32).astype(BF)
        for x in range(SIDE):
            for p, o_ref in enumerate(outs):
                at = (x * len(outs) + p) * rows
                o_ref[x * rows : (x + 1) * rows, :] = out[at : at + rows]

    pl.when(pl.program_id(0) < steps)(lambda: part(own_ref))
    pl.when(pl.program_id(0) >= steps)(lambda: part(other_ref))


def matmul_out(hiddens, own, other, count):
    depth, chans = own.shape
    tokens = SIDE * hiddens[0].shape[0]
    tile = 256
    steps = chans // tile
    return pl.pallas_call(
        mm2_kernel,
        grid=(2 * steps,),
        in_specs=[pl.BlockSpec(memory_space=pl.ANY)] * SIDE
        + [
            pl.BlockSpec((depth, tile), lambda i: (0, jnp.minimum(i, steps - 1))),
            pl.BlockSpec((depth, tile), lambda i: (0, jnp.maximum(i - steps, 0))),
        ],
        out_specs=[pl.BlockSpec((tokens // count, tile), lambda i: (0, i))] * count,
        out_shape=[jax.ShapeDtypeStruct((tokens // count, 2 * chans), BF)] * count,
        scratch_shapes=[pltpu.VMEM((tokens, depth), BF), pltpu.SemaphoreType.DMA((SIDE,))],
        compiler_params=params(58),
        cost_estimate=pl.CostEstimate(
            flops=4 * tokens * depth * chans,
            bytes_accessed=2 * (tokens * depth + 2 * depth * chans + 2 * tokens * chans),
            transcendentals=0,
        ),
    )(*hiddens, own, other)


def pair_kernel(a, b, o):
    o[...] = (a[...].astype(F32) + b[...].astype(F32)).astype(BF)


def add_pair(a, b):
    rows, width = a.shape
    block = pl.BlockSpec((rows // 2, width), lambda j: (j, 0))
    return pl.pallas_call(
        pair_kernel,
        grid=(2,),
        in_specs=[block] * 2,
        out_specs=block,
        out_shape=jax.ShapeDtypeStruct((rows, width), BF),
        compiler_params=params(16),
    )(a, b)


def add_kernel(half, a, b, c, *outs):
    total = a[...].astype(F32) + (b[...].astype(F32) + c[...].astype(F32))
    for s, o_ref in enumerate(outs):
        for x in range(total.shape[0] // (SIDE * half)):
            at = (x * SIDE + s) * half
            o_ref[x * half : (x + 1) * half, :] = total[at : at + half].astype(BF)


def add_pieces(half, *parts):
    rows, width = parts[0].shape
    return pl.pallas_call(
        functools.partial(add_kernel, half),
        grid=(2,),
        in_specs=[pl.BlockSpec((rows // 2, width), lambda j: (j, 0))] * len(parts),
        out_specs=[pl.BlockSpec((rows // SIDE // 2, width), lambda j: (j, 0))] * SIDE,
        out_shape=[jax.ShapeDtypeStruct((rows // SIDE, width), BF)] * SIDE,
        compiler_params=params(24),
    )(*parts)


def sum_kernel(a, b, c, d, own_ref, other_ref):
    chans = own_ref.shape[1]
    total = (a[...].astype(F32) + b[...].astype(F32)) + (c[...].astype(F32) + d[...].astype(F32))
    own_ref[...] = total[:, :chans]
    other_ref[...] = total[:, chans:].astype(BF)


def add_last(parts):
    rows, width = parts[0].shape
    return pl.pallas_call(
        sum_kernel,
        out_shape=[
            jax.ShapeDtypeStruct((rows, width // 2), F32),
            jax.ShapeDtypeStruct((rows, width // 2), BF),
        ],
        compiler_params=params(16),
    )(*parts)


def finish_kernel(place_ref, own1, own2, got1, got2, resid_ref, bias_ref, o_ref):
    half = o_ref.shape[1] // 2
    for i in range(2 * SIDE):
        at = pl.ds(i % SIDE * half, half)
        for k, part in enumerate((own1, own2) if i < SIDE else (got1, got2)):
            to = pl.ds(k * half, half)
            value = part[at, :].astype(F32) + resid_ref[place_ref[i], to, :] + bias_ref[...]
            o_ref[place_ref[i], to, :] = value.astype(BF)


def finish(place, own1, own2, got1, got2, resid, bias):
    return pl.pallas_call(
        finish_kernel,
        in_specs=[pl.BlockSpec(memory_space=pltpu.SMEM)] + [pl.BlockSpec(memory_space=pltpu.VMEM)] * 6,
        out_shape=jax.ShapeDtypeStruct(resid.shape, BF),
        compiler_params=params(16),
    )(place, own1, own2, got1, got2, resid, bias[None])


def exchange(a, axis):
    return lax.all_to_all(a, axis, split_axis=0, concat_axis=0, tiled=True)


def tie_kernel(*refs):
    pass


def tie(values, others):
    count = len(values)
    anywhere = pl.BlockSpec(memory_space=pl.ANY)
    return pl.pallas_call(
        tie_kernel,
        in_specs=[anywhere] * (count + len(others)),
        out_specs=[anywhere] * count,
        out_shape=[jax.ShapeDtypeStruct(v.shape, v.dtype) for v in values],
        input_output_aliases={i: i for i in range(count)},
        compiler_params=params(62),
    )(*values, *others)


def spectral(image, filter_bank, gain_first, early):
    rows_here, width, chans = image.shape
    groups = lax.axis_size("row")
    width_all = chans * lax.axis_size("col")
    tokens = rows_here * width
    one, two, three, four = spectral_tables(rows_here, width, rows_here * groups)
    high = lax.Precision.HIGH
    source = image.astype(F32).reshape(tokens, chans)
    sums, squares = lax.psum(
        (jnp.sum(source, axis=-1), jnp.sum(source * source, axis=-1)), "col"
    )
    mean = sums[:, None] / width_all
    square = squares[:, None] / width_all
    normed = (source - mean) / jnp.sqrt(square - mean * mean + 1e-05) * gain_first
    col = jnp.dot(one, normed, precision=high).astype(BF)
    col = exchange(col.reshape(groups, -1, chans), "row").reshape(-1, chans)
    spec = jnp.dot(two, col.astype(F32), precision=high)
    split = spec.shape[0] // 2
    spec_re, spec_im = spec[:split], spec[split:]
    f_re, f_im = filter_bank[0].reshape(-1, chans), filter_bank[1].reshape(-1, chans)
    filt = jnp.concatenate(
        [f_re * spec_re - f_im * spec_im, f_re * spec_im + f_im * spec_re], axis=0
    )
    back = jnp.dot(three, filt, precision=high).astype(BF)
    back = exchange(back.reshape(groups, -1, chans), "row").reshape(-1, chans)
    (back,) = tie([back], early)
    return source + jnp.dot(four, back.astype(F32), precision=high)


def block_places():
    table = []
    for x in range(SIDE):
        for core in range(2):
            row = []
            for far in (False, True):
                at = core ^ far
                for step in (0, APART[at], OTHER[at], 2):
                    row.append((x + (step if step == 0 else -step)) % SIDE * 2 + at)
            table.append(row)
    return jnp.asarray(np.array(table, np.int32))[lax.axis_index("col")]


def gather_near(a, axis):
    far, *near = [hop(a, axis, (s, s)) for s in (2, 1, -1)]
    return jnp.stack([a, *near, far]).reshape(-1, a.shape[1])


def gather_far(a, axis):
    one, two = hop(a, axis, APART), hop(a, axis, OTHER)
    return [a, one, two, hop(one, axis, APART)]


def gather_both(a, axis):
    one, two = tie([hop(a, axis, APART), hop(a, axis, OTHER)], [])
    return [a, one, two, hop(one, axis, APART)]


def gather_gains(gain):
    pair = jnp.stack([gain, swap_cores(gain)])
    rows = jnp.concatenate(gather_far(pair, "x"))
    table = []
    for x in range(SIDE):
        for core in range(2):
            steps = (0, APART[core], OTHER[core], 2)
            table.append([(x - s) % SIDE * 2 + (core ^ k) for s in steps for k in range(2)])
    places = jnp.asarray(np.array(table, np.int32))[lax.axis_index("col")]
    count = rows.shape[0]
    mine = lax.broadcasted_iota(jnp.int32, (count, count), 0) == places[None, :]
    return jnp.sum(jnp.where(mine[:, :, None], rows[None], 0.0), axis=1)


def reduce_far(outs, large, small, half):
    own, fore, back, far = outs
    far = hop(far, large, OTHER)
    back = hop(back, large, APART)
    fore = hop(add_pair(fore, far), large, OTHER)
    return send_back(add_pieces(half, own, back, fore), small)


def send_back(parts, axis):
    far, *near = [hop(parts[i], axis, (s, s)) for i, s in ((3, 2), (1, -1), (2, 1))]
    return [parts[0], *near, far]


def on_device(image, filter_bank, gain_first, gain_second, w_in, b_in, w_out, b_out):
    rows_here, width, chans = image.shape
    cols = lax.axis_size("col")
    w_in_all = lax.all_gather(w_in, "col", axis=0, tiled=True)
    gains = gather_gains(gain_second)
    resid = spectral(image, filter_bank, gain_first, [gains])
    tokens = rows_here * width
    own = tokens // cols
    half = own // 2
    moved = exchange(resid.astype(BF).reshape(cols, own, chans), "col")
    first, second = normalize(moved, gains, half)
    first, second = gather_near(first, "z"), gather_near(second, "y")
    parts = [gather_far(first, "y"), gather_far(second, "z")]
    hiddens = [gather_both(matmul_in(part, w_in_all, b_in), "x") for part in parts]
    other = swap_cores(w_out)
    sums = []
    for hidden, (large, small) in zip(hiddens, (("y", "z"), ("z", "y"))):
        outs = matmul_out(hidden, w_out, other, SIDE)
        sums.append(add_last(reduce_far(outs, large, small, half)))
    (own1, give1), (own2, give2) = sums
    got1, got2 = swap_cores(give1), swap_cores(give2)
    resid = resid.reshape(cols, own, chans)
    result = finish(block_places(), own1, own2, got1, got2, resid, b_out)
    return result.reshape(rows_here, width, chans)


def solution(mesh):
    placed = (
        P("row", None, "col"),
        P(None, None, "row", "col"),
        P("col"),
        P("col"),
        P("col", "row"),
        P("row"),
        P("row", "col"),
        P("col"),
    )
    return jax.shard_map(
        on_device, mesh=mesh, in_specs=placed, out_specs=P("row", None, "col"), check_vma=False
    )
```

```python
import functools
import math

import jax
import jax.numpy as jnp
import numpy as np
from jax import lax
from jax.experimental import pallas as pl
from jax.experimental.pallas import tpu as pltpu
from jax.sharding import PartitionSpec as P

SIDE = 4
BF = jnp.bfloat16
F32 = jnp.float32
MB = 1 << 20


def angles(count):
    index = np.arange(count)
    turn = (index[:, None] * index[None, :]) % count * (2.0 * math.pi / count)
    return np.cos(turn), np.sin(turn)


def spectral_tables(here, width, height):
    groups = height // here
    per = width // groups
    cos_w, sin_w = angles(width)
    cos_h, sin_h = angles(height)
    eye_r, eye_k = np.eye(here), np.eye(per)
    out = np.stack([cos_w, -sin_w]).reshape(2, width, groups, per)
    one = np.einsum("scqk,rt->qrsktc", out, eye_r).reshape(2 * here * width, here * width)
    turn = np.stack([np.stack([cos_h, sin_h]), np.stack([-sin_h, cos_h])])
    turn = turn.reshape(2, 2, groups, here, height)
    two = np.einsum("uvqrn,kl->unkqrvl", turn, eye_k).reshape(2 * height * per, 2 * height * per)
    back = np.stack([np.stack([cos_h, -sin_h]), np.stack([sin_h, cos_h])])
    back = back.reshape(2, 2, height, groups, here)
    three = np.einsum("uvnqr,kl->qrukvnl", back, eye_k).reshape(2 * height * per, 2 * height * per)
    four = np.einsum("sqkc,rt->rcqtsk", out.transpose(0, 2, 3, 1), eye_r)
    four = four.reshape(here * width, 2 * here * width) / (width * height)
    return [t.astype(np.float32) for t in (one, two, three, four)]


def hop(a, axis, steps):
    pairs = []
    for z in range(SIDE):
        for y in range(SIDE):
            for x in range(SIDE):
                for core, step in enumerate(steps):
                    to = {"z": z, "y": y, "x": x}
                    to[axis] = (to[axis] + step) % SIDE
                    source = ((z * SIDE + y) * SIDE + x) * 2 + core
                    pairs.append((source, ((to["z"] * SIDE + to["y"]) * SIDE + to["x"]) * 2 + core))
    return lax.ppermute(a, ("row", "col"), pairs)


APART = (1, -1)
OTHER = (-1, 1)


def swap_cores(a):
    pairs = [(x * 2 + core, x * 2 + 1 - core) for x in range(SIDE) for core in range(2)]
    return lax.ppermute(a, "col", pairs)


def params(mb):
    return pltpu.CompilerParams(vmem_limit_bytes=mb * MB)


def act_kernel(moved_ref, gain_ref, first_ref, second_ref):
    cols, _, chans = moved_ref.shape
    half = first_ref.shape[0]
    values = moved_ref[...].astype(F32)
    mean = jnp.sum(jnp.sum(values, axis=0), axis=-1, keepdims=True) / (cols * chans)
    square = jnp.sum(jnp.sum(values * values, axis=0), axis=-1, keepdims=True) / (cols * chans)
    scale = 1.0 / jnp.sqrt(square - mean * mean + 1e-05)
    for j in range(cols):
        part = ((values[j] - mean) * scale * gain_ref[j : j + 1, :]).astype(BF)
        first_ref[:, j * chans : (j + 1) * chans] = part[:half]
        second_ref[:, j * chans : (j + 1) * chans] = part[half:]


def normalize(moved, gains, half):
    cols, _, chans = moved.shape
    shape = jax.ShapeDtypeStruct((half, cols * chans), BF)
    return pl.pallas_call(act_kernel, out_shape=(shape, shape), compiler_params=params(16))(moved, gains)


def mm1_kernel(*refs):
    pieces, (w_ref, b_ref, o_ref) = refs[:-3], refs[-3:]
    left = jnp.concatenate([p[...] for p in pieces], axis=0)
    pre = jnp.dot(left, w_ref[...], preferred_element_type=F32) + b_ref[...]
    o_ref[...] = (0.5 * pre * (1.0 + lax.erf(pre * math.sqrt(0.5)))).astype(BF)


def matmul_in(pieces, w, b):
    depth, width = w.shape
    rows = pieces[0].shape[0]
    tokens = len(pieces) * rows
    tile = 256
    return pl.pallas_call(
        mm1_kernel,
        grid=(width // tile,),
        in_specs=[pl.BlockSpec((rows, depth), lambda i: (0, 0)) for _ in pieces]
        + [
            pl.BlockSpec((depth, tile), lambda i: (0, i)),
            pl.BlockSpec((1, tile), lambda i: (0, i)),
        ],
        out_specs=pl.BlockSpec((tokens, tile), lambda i: (0, i)),
        out_shape=jax.ShapeDtypeStruct((tokens, width), BF),
        compiler_params=params(58),
        cost_estimate=pl.CostEstimate(
            flops=2 * tokens * depth * width,
            bytes_accessed=2 * (tokens * depth + depth * width),
            transcendentals=0,
        ),
    )(*pieces, w, b[None])


def fill(sources, target, sems):
    rows = target.shape[0] // len(sources)
    copies = [
        pltpu.make_async_copy(source, target.at[pl.ds(i * rows, rows)], sems.at[i])
        for i, source in enumerate(sources)
    ]

    @pl.when(pl.program_id(0) == 0)
    def _():
        for copy in copies:
            copy.start()
        for copy in copies:
            copy.wait()


def mm2_kernel(*refs):
    hiddens, (own_ref, other_ref) = refs[:SIDE], refs[SIDE : SIDE + 2]
    outs, (left, sems) = refs[SIDE + 2 : -2], refs[-2:]
    fill(hiddens, left, sems)
    steps = pl.num_programs(0) // 2
    rows = outs[0].shape[0] // SIDE

    def part(w_ref):
        out = jnp.dot(left[...], w_ref[...], preferred_element_type=F32).astype(BF)
        for x in range(SIDE):
            for p, o_ref in enumerate(outs):
                at = (x * len(outs) + p) * rows
                o_ref[x * rows : (x + 1) * rows, :] = out[at : at + rows]

    pl.when(pl.program_id(0) < steps)(lambda: part(own_ref))
    pl.when(pl.program_id(0) >= steps)(lambda: part(other_ref))


def matmul_out(hiddens, own, other, count):
    depth, chans = own.shape
    tokens = SIDE * hiddens[0].shape[0]
    tile = 256
    steps = chans // tile
    return pl.pallas_call(
        mm2_kernel,
        grid=(2 * steps,),
        in_specs=[pl.BlockSpec(memory_space=pl.ANY)] * SIDE
        + [
            pl.BlockSpec((depth, tile), lambda i: (0, jnp.minimum(i, steps - 1))),
            pl.BlockSpec((depth, tile), lambda i: (0, jnp.maximum(i - steps, 0))),
        ],
        out_specs=[pl.BlockSpec((tokens // count, tile), lambda i: (0, i))] * count,
        out_shape=[jax.ShapeDtypeStruct((tokens // count, 2 * chans), BF)] * count,
        scratch_shapes=[pltpu.VMEM((tokens, depth), BF), pltpu.SemaphoreType.DMA((SIDE,))],
        compiler_params=params(32),
        cost_estimate=pl.CostEstimate(
            flops=4 * tokens * depth * chans,
            bytes_accessed=2 * (tokens * depth + 2 * depth * chans + 2 * tokens * chans),
            transcendentals=0,
        ),
    )(*hiddens, own, other)


def pair_kernel(a, b, o):
    o[...] = (a[...].astype(F32) + b[...].astype(F32)).astype(BF)


def add_pair(a, b):
    rows, width = a.shape
    block = pl.BlockSpec((rows // 2, width), lambda j: (j, 0))
    return pl.pallas_call(
        pair_kernel,
        grid=(2,),
        in_specs=[block] * 2,
        out_specs=block,
        out_shape=jax.ShapeDtypeStruct((rows, width), BF),
        compiler_params=params(16),
    )(a, b)


def add_kernel(half, a, b, c, *outs):
    total = a[...].astype(F32) + (b[...].astype(F32) + c[...].astype(F32))
    for s, o_ref in enumerate(outs):
        for x in range(total.shape[0] // (SIDE * half)):
            at = (x * SIDE + s) * half
            o_ref[x * half : (x + 1) * half, :] = total[at : at + half].astype(BF)


def add_pieces(half, *parts):
    rows, width = parts[0].shape
    return pl.pallas_call(
        functools.partial(add_kernel, half),
        grid=(2,),
        in_specs=[pl.BlockSpec((rows // 2, width), lambda j: (j, 0))] * len(parts),
        out_specs=[pl.BlockSpec((rows // SIDE // 2, width), lambda j: (j, 0))] * SIDE,
        out_shape=[jax.ShapeDtypeStruct((rows // SIDE, width), BF)] * SIDE,
        compiler_params=params(24),
    )(*parts)


def sum_kernel(a, b, c, d, own_ref, other_ref):
    chans = own_ref.shape[1]
    total = (a[...].astype(F32) + b[...].astype(F32)) + (c[...].astype(F32) + d[...].astype(F32))
    own_ref[...] = total[:, :chans]
    other_ref[...] = total[:, chans:].astype(BF)


def add_last(parts):
    rows, width = parts[0].shape
    return pl.pallas_call(
        sum_kernel,
        out_shape=[
            jax.ShapeDtypeStruct((rows, width // 2), F32),
            jax.ShapeDtypeStruct((rows, width // 2), BF),
        ],
        compiler_params=params(16),
    )(*parts)


def finish_kernel(place_ref, own1, own2, got1, got2, resid_ref, bias_ref, o_ref):
    half = o_ref.shape[1] // 2
    for i in range(2 * SIDE):
        at = pl.ds(i % SIDE * half, half)
        for k, part in enumerate((own1, own2) if i < SIDE else (got1, got2)):
            to = pl.ds(k * half, half)
            value = part[at, :].astype(F32) + resid_ref[place_ref[i], to, :] + bias_ref[...]
            o_ref[place_ref[i], to, :] = value.astype(BF)


def finish(place, own1, own2, got1, got2, resid, bias):
    return pl.pallas_call(
        finish_kernel,
        in_specs=[pl.BlockSpec(memory_space=pltpu.SMEM)] + [pl.BlockSpec(memory_space=pltpu.VMEM)] * 6,
        out_shape=jax.ShapeDtypeStruct(resid.shape, BF),
        compiler_params=params(16),
    )(place, own1, own2, got1, got2, resid, bias[None])


def exchange(a, axis):
    return lax.all_to_all(a, axis, split_axis=0, concat_axis=0, tiled=True)


def tie_kernel(*refs):
    pass


def tie(values, others):
    count = len(values)
    anywhere = pl.BlockSpec(memory_space=pl.ANY)
    return pl.pallas_call(
        tie_kernel,
        in_specs=[anywhere] * (count + len(others)),
        out_specs=[anywhere] * count,
        out_shape=[jax.ShapeDtypeStruct(v.shape, v.dtype) for v in values],
        input_output_aliases={i: i for i in range(count)},
        compiler_params=params(62),
    )(*values, *others)


def spectral(image, filter_bank, gain_first, early):
    rows_here, width, chans = image.shape
    groups = lax.axis_size("row")
    width_all = chans * lax.axis_size("col")
    tokens = rows_here * width
    one, two, three, four = spectral_tables(rows_here, width, rows_here * groups)
    high = lax.Precision.HIGH
    source = image.astype(F32).reshape(tokens, chans)
    sums, squares = lax.psum(
        (jnp.sum(source, axis=-1), jnp.sum(source * source, axis=-1)), "col"
    )
    mean = sums[:, None] / width_all
    square = squares[:, None] / width_all
    normed = (source - mean) / jnp.sqrt(square - mean * mean + 1e-05) * gain_first
    col = jnp.dot(one, normed, precision=high).astype(BF)
    col = exchange(col.reshape(groups, -1, chans), "row").reshape(-1, chans)
    (col,) = tie([col], early)
    spec = jnp.dot(two, col.astype(F32), precision=high)
    split = spec.shape[0] // 2
    spec_re, spec_im = spec[:split], spec[split:]
    f_re, f_im = filter_bank[0].reshape(-1, chans), filter_bank[1].reshape(-1, chans)
    filt = jnp.concatenate(
        [f_re * spec_re - f_im * spec_im, f_re * spec_im + f_im * spec_re], axis=0
    )
    back = jnp.dot(three, filt, precision=high).astype(BF)
    back = exchange(back.reshape(groups, -1, chans), "row").reshape(-1, chans)
    return source + jnp.dot(four, back.astype(F32), precision=high)


def block_places():
    table = []
    for x in range(SIDE):
        for core in range(2):
            row = []
            for far in (False, True):
                at = core ^ far
                for step in (0, APART[at], OTHER[at], 2):
                    row.append((x + (step if step == 0 else -step)) % SIDE * 2 + at)
            table.append(row)
    return jnp.asarray(np.array(table, np.int32))[lax.axis_index("col")]


def gather_near(a, axis):
    far, *near = [hop(a, axis, (s, s)) for s in (2, 1, -1)]
    return jnp.stack([a, *near, far]).reshape(-1, a.shape[1])


def gather_far(a, axis):
    one, two = hop(a, axis, APART), hop(a, axis, OTHER)
    return [a, one, two, hop(one, axis, APART)]


def gather_both(a, axis):
    one, two = tie([hop(a, axis, APART), hop(a, axis, OTHER)], [])
    return [a, one, two, hop(one, axis, APART)]


def gather_gains(gain):
    pair = jnp.stack([gain, swap_cores(gain)])
    rows = jnp.concatenate(gather_far(pair, "x"))
    table = []
    for x in range(SIDE):
        for core in range(2):
            steps = (0, APART[core], OTHER[core], 2)
            table.append([(x - s) % SIDE * 2 + (core ^ k) for s in steps for k in range(2)])
    places = jnp.asarray(np.array(table, np.int32))[lax.axis_index("col")]
    count = rows.shape[0]
    mine = lax.broadcasted_iota(jnp.int32, (count, count), 0) == places[None, :]
    return jnp.sum(jnp.where(mine[:, :, None], rows[None], 0.0), axis=1)


def reduce_far(outs, large, small, half):
    own, fore, back, far = outs
    far = hop(far, large, OTHER)
    back = hop(back, large, APART)
    fore = hop(add_pair(fore, far), large, OTHER)
    return send_back(add_pieces(half, own, back, fore), small)


def send_back(parts, axis):
    far, *near = [hop(parts[i], axis, (s, s)) for i, s in ((3, 2), (1, -1), (2, 1))]
    return [parts[0], *near, far]


def on_device(image, filter_bank, gain_first, gain_second, w_in, b_in, w_out, b_out):
    rows_here, width, chans = image.shape
    cols = lax.axis_size("col")
    w_in_all = lax.all_gather(w_in, "col", axis=0, tiled=True)
    gains = gather_gains(gain_second)
    resid = spectral(image, filter_bank, gain_first, [gains])
    tokens = rows_here * width
    own = tokens // cols
    half = own // 2
    moved = exchange(resid.astype(BF).reshape(cols, own, chans), "col")
    first, second = normalize(moved, gains, half)
    first, second = gather_near(first, "z"), gather_near(second, "y")
    parts = [gather_far(first, "y"), gather_far(second, "z")]
    hiddens = [gather_both(matmul_in(part, w_in_all, b_in), "x") for part in parts]
    other = swap_cores(w_out)
    sums = []
    for hidden, (large, small) in zip(hiddens, (("y", "z"), ("z", "y"))):
        outs = matmul_out(hidden, w_out, other, SIDE)
        sums.append(add_last(reduce_far(outs, large, small, half)))
    (own1, give1), (own2, give2) = sums
    got1, got2 = swap_cores(give1), swap_cores(give2)
    resid = resid.reshape(cols, own, chans)
    result = finish(block_places(), own1, own2, got1, got2, resid, b_out)
    return result.reshape(rows_here, width, chans)


def solution(mesh):
    placed = (
        P("row", None, "col"),
        P(None, None, "row", "col"),
        P("col"),
        P("col"),
        P("col", "row"),
        P("row"),
        P("row", "col"),
        P("col"),
    )
    return jax.shard_map(
        on_device, mesh=mesh, in_specs=placed, out_specs=P("row", None, "col"), check_vma=False
    )
```

```python
import functools
import math

import jax
import jax.numpy as jnp
import numpy as np
from jax import lax
from jax.experimental import pallas as pl
from jax.experimental.pallas import tpu as pltpu
from jax.sharding import PartitionSpec as P

SIDE = 4
BF = jnp.bfloat16
F32 = jnp.float32
MB = 1 << 20


def angles(count):
    index = np.arange(count)
    turn = (index[:, None] * index[None, :]) % count * (2.0 * math.pi / count)
    return np.cos(turn), np.sin(turn)


def spectral_tables(here, width, height):
    groups = height // here
    per = width // groups
    cos_w, sin_w = angles(width)
    cos_h, sin_h = angles(height)
    eye_r, eye_k = np.eye(here), np.eye(per)
    out = np.stack([cos_w, -sin_w]).reshape(2, width, groups, per)
    one = np.einsum("scqk,rt->qrsktc", out, eye_r).reshape(2 * here * width, here * width)
    turn = np.stack([np.stack([cos_h, sin_h]), np.stack([-sin_h, cos_h])])
    turn = turn.reshape(2, 2, groups, here, height)
    two = np.einsum("uvqrn,kl->unkqrvl", turn, eye_k).reshape(2 * height * per, 2 * height * per)
    back = np.stack([np.stack([cos_h, -sin_h]), np.stack([sin_h, cos_h])])
    back = back.reshape(2, 2, height, groups, here)
    three = np.einsum("uvnqr,kl->qrukvnl", back, eye_k).reshape(2 * height * per, 2 * height * per)
    four = np.einsum("sqkc,rt->rcqtsk", out.transpose(0, 2, 3, 1), eye_r)
    four = four.reshape(here * width, 2 * here * width) / (width * height)
    return [t.astype(np.float32) for t in (one, two, three, four)]


def hop(a, axis, steps):
    pairs = []
    for z in range(SIDE):
        for y in range(SIDE):
            for x in range(SIDE):
                for core, step in enumerate(steps):
                    to = {"z": z, "y": y, "x": x}
                    to[axis] = (to[axis] + step) % SIDE
                    source = ((z * SIDE + y) * SIDE + x) * 2 + core
                    pairs.append((source, ((to["z"] * SIDE + to["y"]) * SIDE + to["x"]) * 2 + core))
    return lax.ppermute(a, ("row", "col"), pairs)


APART = (1, -1)
OTHER = (-1, 1)


def swap_cores(a):
    pairs = [(x * 2 + core, x * 2 + 1 - core) for x in range(SIDE) for core in range(2)]
    return lax.ppermute(a, "col", pairs)


def params(mb):
    return pltpu.CompilerParams(vmem_limit_bytes=mb * MB)


def act_kernel(moved_ref, gain_ref, first_ref, second_ref):
    cols, _, chans = moved_ref.shape
    half = first_ref.shape[0]
    values = moved_ref[...].astype(F32)
    mean = jnp.sum(jnp.sum(values, axis=0), axis=-1, keepdims=True) / (cols * chans)
    square = jnp.sum(jnp.sum(values * values, axis=0), axis=-1, keepdims=True) / (cols * chans)
    scale = 1.0 / jnp.sqrt(square - mean * mean + 1e-05)
    for j in range(cols):
        part = ((values[j] - mean) * scale * gain_ref[j : j + 1, :]).astype(BF)
        first_ref[:, j * chans : (j + 1) * chans] = part[:half]
        second_ref[:, j * chans : (j + 1) * chans] = part[half:]


def normalize(moved, gains, half):
    cols, _, chans = moved.shape
    shape = jax.ShapeDtypeStruct((half, cols * chans), BF)
    return pl.pallas_call(act_kernel, out_shape=(shape, shape), compiler_params=params(16))(moved, gains)


def mm1_kernel(*refs):
    pieces, (w_ref, b_ref, o_ref) = refs[:-3], refs[-3:]
    left = jnp.concatenate([p[...] for p in pieces], axis=0)
    pre = jnp.dot(left, w_ref[...], preferred_element_type=F32) + b_ref[...]
    o_ref[...] = (0.5 * pre * (1.0 + lax.erf(pre * math.sqrt(0.5)))).astype(BF)


def matmul_in(pieces, w, b):
    depth, width = w.shape
    rows = pieces[0].shape[0]
    tokens = len(pieces) * rows
    tile = 512
    return pl.pallas_call(
        mm1_kernel,
        grid=(width // tile,),
        in_specs=[pl.BlockSpec((rows, depth), lambda i: (0, 0)) for _ in pieces]
        + [
            pl.BlockSpec((depth, tile), lambda i: (0, i)),
            pl.BlockSpec((1, tile), lambda i: (0, i)),
        ],
        out_specs=pl.BlockSpec((tokens, tile), lambda i: (0, i)),
        out_shape=jax.ShapeDtypeStruct((tokens, width), BF),
        compiler_params=params(58),
        cost_estimate=pl.CostEstimate(
            flops=2 * tokens * depth * width,
            bytes_accessed=2 * (tokens * depth + depth * width),
            transcendentals=0,
        ),
    )(*pieces, w, b[None])


def fill(sources, target, sems):
    rows = target.shape[0] // len(sources)
    copies = [
        pltpu.make_async_copy(source, target.at[pl.ds(i * rows, rows)], sems.at[i])
        for i, source in enumerate(sources)
    ]

    @pl.when(pl.program_id(0) == 0)
    def _():
        for copy in copies:
            copy.start()
        for copy in copies:
            copy.wait()


def mm2_kernel(*refs):
    hiddens, (own_ref, other_ref) = refs[:SIDE], refs[SIDE : SIDE + 2]
    outs, (left, sems) = refs[SIDE + 2 : -2], refs[-2:]
    fill(hiddens, left, sems)
    steps = pl.num_programs(0) // 2
    rows = outs[0].shape[0] // SIDE

    def part(w_ref):
        out = jnp.dot(left[...], w_ref[...], preferred_element_type=F32).astype(BF)
        for x in range(SIDE):
            for p, o_ref in enumerate(outs):
                at = (x * len(outs) + p) * rows
                o_ref[x * rows : (x + 1) * rows, :] = out[at : at + rows]

    pl.when(pl.program_id(0) < steps)(lambda: part(own_ref))
    pl.when(pl.program_id(0) >= steps)(lambda: part(other_ref))


def matmul_out(hiddens, own, other, count):
    depth, chans = own.shape
    tokens = SIDE * hiddens[0].shape[0]
    tile = 256
    steps = chans // tile
    return pl.pallas_call(
        mm2_kernel,
        grid=(2 * steps,),
        in_specs=[pl.BlockSpec(memory_space=pl.ANY)] * SIDE
        + [
            pl.BlockSpec((depth, tile), lambda i: (0, jnp.minimum(i, steps - 1))),
            pl.BlockSpec((depth, tile), lambda i: (0, jnp.maximum(i - steps, 0))),
        ],
        out_specs=[pl.BlockSpec((tokens // count, tile), lambda i: (0, i))] * count,
        out_shape=[jax.ShapeDtypeStruct((tokens // count, 2 * chans), BF)] * count,
        scratch_shapes=[pltpu.VMEM((tokens, depth), BF), pltpu.SemaphoreType.DMA((SIDE,))],
        compiler_params=params(32),
        cost_estimate=pl.CostEstimate(
            flops=4 * tokens * depth * chans,
            bytes_accessed=2 * (tokens * depth + 2 * depth * chans + 2 * tokens * chans),
            transcendentals=0,
        ),
    )(*hiddens, own, other)


def pair_kernel(a, b, o):
    o[...] = (a[...].astype(F32) + b[...].astype(F32)).astype(BF)


def add_pair(a, b):
    rows, width = a.shape
    block = pl.BlockSpec((rows // 2, width), lambda j: (j, 0))
    return pl.pallas_call(
        pair_kernel,
        grid=(2,),
        in_specs=[block] * 2,
        out_specs=block,
        out_shape=jax.ShapeDtypeStruct((rows, width), BF),
        compiler_params=params(16),
    )(a, b)


def add_kernel(half, a, b, c, *outs):
    total = a[...].astype(F32) + (b[...].astype(F32) + c[...].astype(F32))
    for s, o_ref in enumerate(outs):
        for x in range(total.shape[0] // (SIDE * half)):
            at = (x * SIDE + s) * half
            o_ref[x * half : (x + 1) * half, :] = total[at : at + half].astype(BF)


def add_pieces(half, *parts):
    rows, width = parts[0].shape
    return pl.pallas_call(
        functools.partial(add_kernel, half),
        grid=(2,),
        in_specs=[pl.BlockSpec((rows // 2, width), lambda j: (j, 0))] * len(parts),
        out_specs=[pl.BlockSpec((rows // SIDE // 2, width), lambda j: (j, 0))] * SIDE,
        out_shape=[jax.ShapeDtypeStruct((rows // SIDE, width), BF)] * SIDE,
        compiler_params=params(24),
    )(*parts)


def sum_kernel(a, b, c, d, own_ref, other_ref):
    chans = own_ref.shape[1]
    total = (a[...].astype(F32) + b[...].astype(F32)) + (c[...].astype(F32) + d[...].astype(F32))
    own_ref[...] = total[:, :chans]
    other_ref[...] = total[:, chans:].astype(BF)


def add_last(parts):
    rows, width = parts[0].shape
    return pl.pallas_call(
        sum_kernel,
        out_shape=[
            jax.ShapeDtypeStruct((rows, width // 2), F32),
            jax.ShapeDtypeStruct((rows, width // 2), BF),
        ],
        compiler_params=params(16),
    )(*parts)


def finish_kernel(place_ref, own1, own2, got1, got2, resid_ref, bias_ref, o_ref):
    half = o_ref.shape[1] // 2
    for i in range(2 * SIDE):
        at = pl.ds(i % SIDE * half, half)
        for k, part in enumerate((own1, own2) if i < SIDE else (got1, got2)):
            to = pl.ds(k * half, half)
            value = part[at, :].astype(F32) + resid_ref[place_ref[i], to, :] + bias_ref[...]
            o_ref[place_ref[i], to, :] = value.astype(BF)


def finish(place, own1, own2, got1, got2, resid, bias):
    return pl.pallas_call(
        finish_kernel,
        in_specs=[pl.BlockSpec(memory_space=pltpu.SMEM)] + [pl.BlockSpec(memory_space=pltpu.VMEM)] * 6,
        out_shape=jax.ShapeDtypeStruct(resid.shape, BF),
        compiler_params=params(16),
    )(place, own1, own2, got1, got2, resid, bias[None])


def exchange(a, axis):
    return lax.all_to_all(a, axis, split_axis=0, concat_axis=0, tiled=True)


def tie_kernel(*refs):
    pass


def tie(values, others):
    count = len(values)
    anywhere = pl.BlockSpec(memory_space=pl.ANY)
    return pl.pallas_call(
        tie_kernel,
        in_specs=[anywhere] * (count + len(others)),
        out_specs=[anywhere] * count,
        out_shape=[jax.ShapeDtypeStruct(v.shape, v.dtype) for v in values],
        input_output_aliases={i: i for i in range(count)},
        compiler_params=params(62),
    )(*values, *others)


def spectral(image, filter_bank, gain_first, early):
    rows_here, width, chans = image.shape
    groups = lax.axis_size("row")
    width_all = chans * lax.axis_size("col")
    tokens = rows_here * width
    one, two, three, four = spectral_tables(rows_here, width, rows_here * groups)
    high = lax.Precision.HIGH
    source = image.astype(F32).reshape(tokens, chans)
    sums, squares = lax.psum(
        (jnp.sum(source, axis=-1), jnp.sum(source * source, axis=-1)), "col"
    )
    mean = sums[:, None] / width_all
    square = squares[:, None] / width_all
    normed = (source - mean) / jnp.sqrt(square - mean * mean + 1e-05) * gain_first
    col = jnp.dot(one, normed, precision=high).astype(BF)
    col = exchange(col.reshape(groups, -1, chans), "row").reshape(-1, chans)
    spec = jnp.dot(two, col.astype(F32), precision=high)
    split = spec.shape[0] // 2
    spec_re, spec_im = spec[:split], spec[split:]
    f_re, f_im = filter_bank[0].reshape(-1, chans), filter_bank[1].reshape(-1, chans)
    filt = jnp.concatenate(
        [f_re * spec_re - f_im * spec_im, f_re * spec_im + f_im * spec_re], axis=0
    )
    back = jnp.dot(three, filt, precision=high).astype(BF)
    back = exchange(back.reshape(groups, -1, chans), "row").reshape(-1, chans)
    back, *early = tie([back, *early], [])
    return source + jnp.dot(four, back.astype(F32), precision=high), early


def block_places():
    table = []
    for x in range(SIDE):
        for core in range(2):
            row = []
            for far in (False, True):
                at = core ^ far
                for step in (0, APART[at], OTHER[at], 2):
                    row.append((x + (step if step == 0 else -step)) % SIDE * 2 + at)
            table.append(row)
    return jnp.asarray(np.array(table, np.int32))[lax.axis_index("col")]


def gather_near(a, axis):
    far, *near = [hop(a, axis, (s, s)) for s in (2, 1, -1)]
    return jnp.stack([a, *near, far]).reshape(-1, a.shape[1])


def gather_far(a, axis):
    one, two = hop(a, axis, APART), hop(a, axis, OTHER)
    return [a, one, two, hop(one, axis, APART)]


def gather_gains(gain):
    return gather_far(jnp.stack([gain, swap_cores(gain)]), "x")


def place_gains(parts):
    rows = jnp.concatenate(parts)
    table = []
    for x in range(SIDE):
        for core in range(2):
            steps = (0, APART[core], OTHER[core], 2)
            table.append([(x - s) % SIDE * 2 + (core ^ k) for s in steps for k in range(2)])
    places = jnp.asarray(np.array(table, np.int32))[lax.axis_index("col")]
    count = rows.shape[0]
    mine = lax.broadcasted_iota(jnp.int32, (count, count), 0) == places[None, :]
    return jnp.sum(jnp.where(mine[:, :, None], rows[None], 0.0), axis=1)


def reduce_far(outs, large, small, half):
    own, fore, back, far = outs
    far = hop(far, large, OTHER)
    back = hop(back, large, APART)
    fore = hop(add_pair(fore, far), large, OTHER)
    return send_back(add_pieces(half, own, back, fore), small)


def send_back(parts, axis):
    far, *near = [hop(parts[i], axis, (s, s)) for i, s in ((3, 2), (1, -1), (2, 1))]
    return [parts[0], *near, far]


def on_device(image, filter_bank, gain_first, gain_second, w_in, b_in, w_out, b_out):
    rows_here, width, chans = image.shape
    cols = lax.axis_size("col")
    w_in_all = lax.all_gather(w_in, "col", axis=0, tiled=True)
    gains = gather_gains(gain_second)
    resid, gains = spectral(image, filter_bank, gain_first, gains)
    tokens = rows_here * width
    own = tokens // cols
    half = own // 2
    moved = exchange(resid.astype(BF).reshape(cols, own, chans), "col")
    first, second = normalize(moved, place_gains(gains), half)
    first, second = gather_near(first, "z"), gather_near(second, "y")
    parts = [gather_far(first, "y"), gather_far(second, "z")]
    hiddens = [gather_far(matmul_in(part, w_in_all, b_in), "x") for part in parts]
    other = swap_cores(w_out)
    sums = []
    for hidden, (large, small) in zip(hiddens, (("y", "z"), ("z", "y"))):
        outs = matmul_out(hidden, w_out, other, SIDE)
        sums.append(add_last(reduce_far(outs, large, small, half)))
    (own1, give1), (own2, give2) = sums
    got1, got2 = swap_cores(give1), swap_cores(give2)
    resid = resid.reshape(cols, own, chans)
    result = finish(block_places(), own1, own2, got1, got2, resid, b_out)
    return result.reshape(rows_here, width, chans)


def solution(mesh):
    placed = (
        P("row", None, "col"),
        P(None, None, "row", "col"),
        P("col"),
        P("col"),
        P("col", "row"),
        P("row"),
        P("row", "col"),
        P("col"),
    )
    return jax.shard_map(
        on_device, mesh=mesh, in_specs=placed, out_specs=P("row", None, "col"), check_vma=False
    )
```

```python
import functools
import math

import jax
import jax.numpy as jnp
import numpy as np
from jax import lax
from jax.experimental import pallas as pl
from jax.experimental.pallas import tpu as pltpu
from jax.sharding import PartitionSpec as P

SIDE = 4
BF = jnp.bfloat16
F32 = jnp.float32
MB = 1 << 20


def angles(count):
    index = np.arange(count)
    turn = (index[:, None] * index[None, :]) % count * (2.0 * math.pi / count)
    return np.cos(turn), np.sin(turn)


def spectral_tables(here, width, height):
    groups = height // here
    per = width // groups
    cos_w, sin_w = angles(width)
    cos_h, sin_h = angles(height)
    eye_r, eye_k = np.eye(here), np.eye(per)
    out = np.stack([cos_w, -sin_w]).reshape(2, width, groups, per)
    one = np.einsum("scqk,rt->qrsktc", out, eye_r).reshape(2 * here * width, here * width)
    turn = np.stack([np.stack([cos_h, sin_h]), np.stack([-sin_h, cos_h])])
    turn = turn.reshape(2, 2, groups, here, height)
    two = np.einsum("uvqrn,kl->unkqrvl", turn, eye_k).reshape(2 * height * per, 2 * height * per)
    back = np.stack([np.stack([cos_h, -sin_h]), np.stack([sin_h, cos_h])])
    back = back.reshape(2, 2, height, groups, here)
    three = np.einsum("uvnqr,kl->qrukvnl", back, eye_k).reshape(2 * height * per, 2 * height * per)
    four = np.einsum("sqkc,rt->rcqtsk", out.transpose(0, 2, 3, 1), eye_r)
    four = four.reshape(here * width, 2 * here * width) / (width * height)
    return [t.astype(np.float32) for t in (one, two, three, four)]


def hop(a, axis, steps):
    pairs = []
    for z in range(SIDE):
        for y in range(SIDE):
            for x in range(SIDE):
                for core, step in enumerate(steps):
                    to = {"z": z, "y": y, "x": x}
                    to[axis] = (to[axis] + step) % SIDE
                    source = ((z * SIDE + y) * SIDE + x) * 2 + core
                    pairs.append((source, ((to["z"] * SIDE + to["y"]) * SIDE + to["x"]) * 2 + core))
    return lax.ppermute(a, ("row", "col"), pairs)


APART = (1, -1)
OTHER = (-1, 1)


def swap_cores(a):
    pairs = [(x * 2 + core, x * 2 + 1 - core) for x in range(SIDE) for core in range(2)]
    return lax.ppermute(a, "col", pairs)


def params(mb):
    return pltpu.CompilerParams(vmem_limit_bytes=mb * MB)


def act_kernel(moved_ref, gain_ref, first_ref, second_ref):
    cols, _, chans = moved_ref.shape
    half = first_ref.shape[0]
    values = moved_ref[...].astype(F32)
    mean = jnp.sum(jnp.sum(values, axis=0), axis=-1, keepdims=True) / (cols * chans)
    square = jnp.sum(jnp.sum(values * values, axis=0), axis=-1, keepdims=True) / (cols * chans)
    scale = 1.0 / jnp.sqrt(square - mean * mean + 1e-05)
    for j in range(cols):
        part = ((values[j] - mean) * scale * gain_ref[j : j + 1, :]).astype(BF)
        first_ref[:, j * chans : (j + 1) * chans] = part[:half]
        second_ref[:, j * chans : (j + 1) * chans] = part[half:]


def normalize(moved, gains, half):
    cols, _, chans = moved.shape
    shape = jax.ShapeDtypeStruct((half, cols * chans), BF)
    return pl.pallas_call(act_kernel, out_shape=(shape, shape), compiler_params=params(16))(moved, gains)


def mm1_kernel(*refs):
    pieces, (w_ref, b_ref, o_ref) = refs[:-3], refs[-3:]
    left = jnp.concatenate([p[...] for p in pieces], axis=0)
    pre = jnp.dot(left, w_ref[...], preferred_element_type=F32) + b_ref[...]
    o_ref[...] = (0.5 * pre * (1.0 + lax.erf(pre * math.sqrt(0.5)))).astype(BF)


def matmul_in(pieces, w, b):
    depth, width = w.shape
    rows = pieces[0].shape[0]
    tokens = len(pieces) * rows
    tile = 512
    return pl.pallas_call(
        mm1_kernel,
        grid=(width // tile,),
        in_specs=[pl.BlockSpec((rows, depth), lambda i: (0, 0)) for _ in pieces]
        + [
            pl.BlockSpec((depth, tile), lambda i: (0, i)),
            pl.BlockSpec((1, tile), lambda i: (0, i)),
        ],
        out_specs=pl.BlockSpec((tokens, tile), lambda i: (0, i)),
        out_shape=jax.ShapeDtypeStruct((tokens, width), BF),
        compiler_params=params(58),
        cost_estimate=pl.CostEstimate(
            flops=2 * tokens * depth * width,
            bytes_accessed=2 * (tokens * depth + depth * width),
            transcendentals=0,
        ),
    )(*pieces, w, b[None])


def fill(sources, target, sems):
    rows = target.shape[0] // len(sources)
    copies = [
        pltpu.make_async_copy(source, target.at[pl.ds(i * rows, rows)], sems.at[i])
        for i, source in enumerate(sources)
    ]

    @pl.when(pl.program_id(0) == 0)
    def _():
        for copy in copies:
            copy.start()
        for copy in copies:
            copy.wait()


def mm2_kernel(*refs):
    hiddens, (own_ref, other_ref) = refs[:SIDE], refs[SIDE : SIDE + 2]
    outs, (left, sems) = refs[SIDE + 2 : -2], refs[-2:]
    fill(hiddens, left, sems)
    steps = pl.num_programs(0) // 2
    rows = outs[0].shape[0] // SIDE

    def part(w_ref):
        out = jnp.dot(left[...], w_ref[...], preferred_element_type=F32).astype(BF)
        for x in range(SIDE):
            for p, o_ref in enumerate(outs):
                at = (x * len(outs) + p) * rows
                o_ref[x * rows : (x + 1) * rows, :] = out[at : at + rows]

    pl.when(pl.program_id(0) < steps)(lambda: part(own_ref))
    pl.when(pl.program_id(0) >= steps)(lambda: part(other_ref))


def matmul_out(hiddens, own, other, count):
    depth, chans = own.shape
    tokens = SIDE * hiddens[0].shape[0]
    tile = 256
    steps = chans // tile
    return pl.pallas_call(
        mm2_kernel,
        grid=(2 * steps,),
        in_specs=[pl.BlockSpec(memory_space=pl.ANY)] * SIDE
        + [
            pl.BlockSpec((depth, tile), lambda i: (0, jnp.minimum(i, steps - 1))),
            pl.BlockSpec((depth, tile), lambda i: (0, jnp.maximum(i - steps, 0))),
        ],
        out_specs=[pl.BlockSpec((tokens // count, tile), lambda i: (0, i))] * count,
        out_shape=[jax.ShapeDtypeStruct((tokens // count, 2 * chans), BF)] * count,
        scratch_shapes=[pltpu.VMEM((tokens, depth), BF), pltpu.SemaphoreType.DMA((SIDE,))],
        compiler_params=params(32),
        cost_estimate=pl.CostEstimate(
            flops=4 * tokens * depth * chans,
            bytes_accessed=2 * (tokens * depth + 2 * depth * chans + 2 * tokens * chans),
            transcendentals=0,
        ),
    )(*hiddens, own, other)


def pair_kernel(a, b, o):
    o[...] = (a[...].astype(F32) + b[...].astype(F32)).astype(BF)


def add_pair(a, b):
    rows, width = a.shape
    block = pl.BlockSpec((rows // 2, width), lambda j: (j, 0))
    return pl.pallas_call(
        pair_kernel,
        grid=(2,),
        in_specs=[block] * 2,
        out_specs=block,
        out_shape=jax.ShapeDtypeStruct((rows, width), BF),
        compiler_params=params(16),
    )(a, b)


def add_kernel(half, a, b, c, *outs):
    total = a[...].astype(F32) + (b[...].astype(F32) + c[...].astype(F32))
    for s, o_ref in enumerate(outs):
        for x in range(total.shape[0] // (SIDE * half)):
            at = (x * SIDE + s) * half
            o_ref[x * half : (x + 1) * half, :] = total[at : at + half].astype(BF)


def add_pieces(half, *parts):
    rows, width = parts[0].shape
    return pl.pallas_call(
        functools.partial(add_kernel, half),
        grid=(2,),
        in_specs=[pl.BlockSpec((rows // 2, width), lambda j: (j, 0))] * len(parts),
        out_specs=[pl.BlockSpec((rows // SIDE // 2, width), lambda j: (j, 0))] * SIDE,
        out_shape=[jax.ShapeDtypeStruct((rows // SIDE, width), BF)] * SIDE,
        compiler_params=params(24),
    )(*parts)


def sum_kernel(a, b, c, d, own_ref, other_ref):
    chans = own_ref.shape[1]
    total = (a[...].astype(F32) + b[...].astype(F32)) + (c[...].astype(F32) + d[...].astype(F32))
    own_ref[...] = total[:, :chans]
    other_ref[...] = total[:, chans:].astype(BF)


def add_last(parts):
    rows, width = parts[0].shape
    return pl.pallas_call(
        sum_kernel,
        out_shape=[
            jax.ShapeDtypeStruct((rows, width // 2), F32),
            jax.ShapeDtypeStruct((rows, width // 2), BF),
        ],
        compiler_params=params(16),
    )(*parts)


def finish_kernel(place_ref, own1, own2, got1, got2, resid_ref, bias_ref, o_ref):
    half = o_ref.shape[1] // 2
    for i in range(2 * SIDE):
        at = pl.ds(i % SIDE * half, half)
        for k, part in enumerate((own1, own2) if i < SIDE else (got1, got2)):
            to = pl.ds(k * half, half)
            value = part[at, :].astype(F32) + resid_ref[place_ref[i], to, :] + bias_ref[...]
            o_ref[place_ref[i], to, :] = value.astype(BF)


def finish(place, own1, own2, got1, got2, resid, bias):
    return pl.pallas_call(
        finish_kernel,
        in_specs=[pl.BlockSpec(memory_space=pltpu.SMEM)] + [pl.BlockSpec(memory_space=pltpu.VMEM)] * 6,
        out_shape=jax.ShapeDtypeStruct(resid.shape, BF),
        compiler_params=params(16),
    )(place, own1, own2, got1, got2, resid, bias[None])


def exchange(a, axis):
    return lax.all_to_all(a, axis, split_axis=0, concat_axis=0, tiled=True)


def tie_kernel(*refs):
    pass


def tie(values, others):
    count = len(values)
    anywhere = pl.BlockSpec(memory_space=pl.ANY)
    return pl.pallas_call(
        tie_kernel,
        in_specs=[anywhere] * (count + len(others)),
        out_specs=[anywhere] * count,
        out_shape=[jax.ShapeDtypeStruct(v.shape, v.dtype) for v in values],
        input_output_aliases={i: i for i in range(count)},
        compiler_params=params(62),
    )(*values, *others)


def spectral(image, filter_bank, gain_first, early):
    rows_here, width, chans = image.shape
    groups = lax.axis_size("row")
    width_all = chans * lax.axis_size("col")
    tokens = rows_here * width
    one, two, three, four = spectral_tables(rows_here, width, rows_here * groups)
    high = lax.Precision.HIGH
    source = image.astype(F32).reshape(tokens, chans)
    sums, squares = lax.psum(
        (jnp.sum(source, axis=-1), jnp.sum(source * source, axis=-1)), "col"
    )
    mean = sums[:, None] / width_all
    square = squares[:, None] / width_all
    normed = (source - mean) / jnp.sqrt(square - mean * mean + 1e-05) * gain_first
    col = jnp.dot(one, normed, precision=high).astype(BF)
    col = exchange(col.reshape(groups, -1, chans), "row").reshape(-1, chans)
    (col,) = tie([col], early)
    spec = jnp.dot(two, col.astype(F32), precision=high)
    split = spec.shape[0] // 2
    spec_re, spec_im = spec[:split], spec[split:]
    f_re, f_im = filter_bank[0].reshape(-1, chans), filter_bank[1].reshape(-1, chans)
    filt = jnp.concatenate(
        [f_re * spec_re - f_im * spec_im, f_re * spec_im + f_im * spec_re], axis=0
    )
    back = jnp.dot(three, filt, precision=high).astype(BF)
    back = exchange(back.reshape(groups, -1, chans), "row").reshape(-1, chans)
    return source + jnp.dot(four, back.astype(F32), precision=high)


def block_places():
    table = []
    for x in range(SIDE):
        for core in range(2):
            row = []
            for far in (False, True):
                at = core ^ far
                for step in (0, APART[at], OTHER[at], 2):
                    row.append((x + (step if step == 0 else -step)) % SIDE * 2 + at)
            table.append(row)
    return jnp.asarray(np.array(table, np.int32))[lax.axis_index("col")]


def gather_near(a, axis):
    far, *near = [hop(a, axis, (s, s)) for s in (2, 1, -1)]
    return jnp.stack([a, *near, far]).reshape(-1, a.shape[1])


def gather_far(a, axis):
    one, two = hop(a, axis, APART), hop(a, axis, OTHER)
    return [a, one, two, hop(one, axis, APART)]


def gather_gains(gain):
    pair = jnp.stack([gain, swap_cores(gain)])
    rows = jnp.concatenate(gather_far(pair, "x"))
    table = []
    for x in range(SIDE):
        for core in range(2):
            steps = (0, APART[core], OTHER[core], 2)
            table.append([(x - s) % SIDE * 2 + (core ^ k) for s in steps for k in range(2)])
    places = jnp.asarray(np.array(table, np.int32))[lax.axis_index("col")]
    count = rows.shape[0]
    mine = lax.broadcasted_iota(jnp.int32, (count, count), 0) == places[None, :]
    return jnp.sum(jnp.where(mine[:, :, None], rows[None], 0.0), axis=1)


def reduce_far(outs, large, small, half):
    own, fore, back, far = outs
    far = hop(far, large, OTHER)
    back = hop(back, large, APART)
    fore = hop(add_pair(fore, far), large, OTHER)
    return send_back(add_pieces(half, own, back, fore), small)


def send_back(parts, axis):
    far, *near = [hop(parts[i], axis, (s, s)) for i, s in ((3, 2), (1, -1), (2, 1))]
    return [parts[0], *near, far]


def on_device(image, filter_bank, gain_first, gain_second, w_in, b_in, w_out, b_out):
    rows_here, width, chans = image.shape
    cols = lax.axis_size("col")
    w_in_all = lax.all_gather(w_in, "col", axis=0, tiled=True)
    gains = gather_gains(gain_second)
    resid = spectral(image, filter_bank, gain_first, [gains])
    tokens = rows_here * width
    own = tokens // cols
    half = own // 2
    moved = exchange(resid.astype(BF).reshape(cols, own, chans), "col")
    first, second = normalize(moved, gains, half)
    first, second = gather_near(first, "z"), gather_near(second, "y")
    parts = [gather_far(first, "y"), gather_far(second, "z")]
    hiddens = [gather_far(matmul_in(part, w_in_all, b_in), "x") for part in parts]
    other = swap_cores(w_out)
    sums = []
    for hidden, (large, small) in zip(hiddens, (("y", "z"), ("z", "y"))):
        outs = matmul_out(hidden, w_out, other, SIDE)
        sums.append(add_last(reduce_far(outs, large, small, half)))
    (own1, give1), (own2, give2) = sums
    got1, got2 = swap_cores(give1), swap_cores(give2)
    resid = resid.reshape(cols, own, chans)
    result = finish(block_places(), own1, own2, got1, got2, resid, b_out)
    return result.reshape(rows_here, width, chans)


def solution(mesh):
    placed = (
        P("row", None, "col"),
        P(None, None, "row", "col"),
        P("col"),
        P("col"),
        P("col", "row"),
        P("row"),
        P("row", "col"),
        P("col"),
    )
    return jax.shard_map(
        on_device, mesh=mesh, in_specs=placed, out_specs=P("row", None, "col"), check_vma=False
    )
```
